512 devices in a mesh: dp: 8 (over z_lo), tm: 16 (over z_hi, x, core), mp: 4 (over y).
Axes of the slice: x: 4, y: 4, z: 16 (z_hi: 2, z_lo: 8; z = z_hi * 8 + z_lo), core: 2. Of those that a mesh axis runs over, the one named last changes fastest.
Arguments:
- waveform: float32 [8, 2621440], P('dp', ('tm', 'mp')), may hold values from -6 to 6
- lengths: int32 [8], P('dp'), may hold values from 327680 to 2621440, as said below
- sub_weight: bfloat16 [896, 1536], P(('dp', 'tm'), 'mp'), may hold values from -0.1875 to 0.1875
- value_weight: bfloat16 [1536, 1536], P(('dp', 'tm'), 'mp'), may hold values from -0.15625 to 0.15625
- gate_weight: bfloat16 [1536, 1536], P(('dp', 'tm'), 'mp'), may hold values from -0.15625 to 0.15625
- out_weight: bfloat16 [1536, 1536], P('mp', ('dp', 'tm')), may hold values from -0.15625 to 0.15625
- depth_kernel: float32 [31, 1536], P(None, 'mp'), may hold values from -1 to 1
- norm_scale: float32 [1536], P('mp'), may hold values from 0.5 to 2
- norm_shift: float32 [1536], P('mp'), may hold values from -3 to 3
Outputs:
- encoded: bfloat16 [8, 4096, 1536], P('dp', 'tm', 'mp')
The draws below stay inside these ranges and needn't reach their ends.
Inputs may be any that keep to these rules, and one draw needn't show every extreme that they name: `lengths`: in every draw one utterance has exactly 2621440 valid samples.
All inputs are finite; a program needn't handle non-finite values.
Results may differ from the reference program's by a relative error of at most 0.013.
Values may be sent and summed in bfloat16 or wider, within the bound.
A program may use at most 64 MiB of HBM per device.

```python
import math
import jax
import jax.numpy as jnp
from jax import lax

D = 1536
MEL = 128
WIN = 400
HOP = 160
STRIDE = 4
TAPS = 7
KERNEL = 31
BINS = 201
FRAMES = 4096
SAMPLES = 2621440
B = 8
N_MP = 4


def draw_lengths(key, part):
    key = jax.random.fold_in(key, 11)
    number = B
    drawn = jax.random.randint(jax.random.fold_in(key, 1), (number,), SAMPLES // 8, SAMPLES + 1)
    longest = jax.random.randint(jax.random.fold_in(key, 2), (), 0, number)
    position = jnp.arange(number, dtype=jnp.int32)
    drawn = jnp.where(position == longest, SAMPLES, drawn)
    return drawn.astype(jnp.int32)


def block_scale(rng, dims, split, least, largest):
    def one(axis_at, shards_of):
        draws = jax.random.uniform(jax.random.fold_in(jax.random.fold_in(rng, 6), axis_at), (shards_of,), jnp.float32, least / len(split), largest / len(split))
        return jnp.repeat(jnp.exp(draws), dims[axis_at] // shards_of).reshape((-1,) + (1,) * (len(dims) - axis_at - 1))

    factor_of = one(*split[0])
    for cut in split[1:]:
        factor_of = factor_of * one(*cut)
    return factor_of


def normal_values(rng, dims, scale, most, pieces=(), held_as=jnp.bfloat16):
    factor_of = block_scale(rng, dims, pieces, -0.22, 0.18) if pieces else 1.0
    array = jax.random.normal(rng, dims, jnp.float32) * scale * factor_of
    return jnp.minimum(jnp.maximum(array, -most), most).astype(held_as)


def setup_inputs(seed: int = 0) -> dict:
    seeds = jax.random.split(jax.random.key(seed), 10)
    return {
        "waveform": normal_values(seeds[0], (B, SAMPLES), 1.0, 6.0, ((0, 8), (1, 64)), jnp.float32),
        "lengths": draw_lengths(jax.random.fold_in(seeds[9], 71), 0),
        "sub_weight": normal_values(seeds[2], (TAPS * MEL, D), (TAPS * MEL) ** -0.5, 0.1875, ((0, 128), (1, 4))),
        "value_weight": normal_values(seeds[3], (D, D), D ** -0.5, 0.15625, ((0, 128), (1, 4))),
        "gate_weight": normal_values(seeds[4], (D, D), D ** -0.5, 0.15625, ((0, 128), (1, 4))),
        "out_weight": normal_values(seeds[5], (D, D), D ** -0.5, 0.15625, ((0, 4), (1, 128))),
        "depth_kernel": normal_values(seeds[6], (KERNEL, D), KERNEL ** -0.5, 1.0, ((1, 4),), jnp.float32),
        "norm_scale": jnp.clip(jnp.exp(math.log(2.0) - 1.3862944 * jax.random.uniform(seeds[7], (D,), jnp.float32) ** block_scale(seeds[7], (D,), ((0, 4),), -0.2, 0.2)), 0.5, 2.0),
        "norm_shift": normal_values(seeds[8], (D,), 0.5, 3.0, ((0, 4),), jnp.float32),
    }


def mel_filters(bin_count, band_count, frame_width):
    mel_top = 2595.0 * math.log10(1.0 + 8000.0 / 700.0)
    border_list = [700.0 * (10.0 ** (band_index * mel_top / (band_count + 1) / 2595.0) - 1.0) * frame_width / 16000.0 for band_index in range(band_count + 2)]
    borders = jnp.asarray(border_list, dtype=jnp.float32)
    centers = jnp.arange(bin_count, dtype=jnp.float32)[:, None]
    middle = borders[1:-1][None, :]
    lower_edge = jnp.minimum(borders[:-2], borders[1:-1] - 1.0)[None, :]
    upper_edge = jnp.maximum(borders[2:], borders[1:-1] + 1.0)[None, :]
    rising = (centers - lower_edge) / (middle - lower_edge)
    falling = (upper_edge - centers) / (upper_edge - middle)
    return jnp.maximum(0.0, jnp.minimum(rising, falling)).astype(jnp.float32)

def hann_window(width):
    phases = jnp.arange(width, dtype=jnp.float32) * (2.0 * math.pi / width)
    return 0.5 - 0.5 * jnp.cos(phases)

def log_mel(samples, length):
    sample_count = samples.shape[0]
    position = jnp.arange(sample_count, dtype=jnp.int32)
    masked = jnp.where(position < length, samples, jnp.float32(0.0))
    padded = jnp.concatenate([masked, jnp.zeros((2 * HOP,), masked.dtype)])
    blocks = padded.reshape(-1, HOP)
    mel_count = sample_count // HOP
    frames = jnp.concatenate([blocks[:mel_count], blocks[1:mel_count + 1], blocks[2:mel_count + 2, :WIN - 2 * HOP]], axis=1)
    spectrum = jnp.fft.rfft(frames * hann_window(WIN), axis=1)
    power_bins = jnp.real(spectrum) ** 2 + jnp.imag(spectrum) ** 2
    filters = mel_filters(BINS, MEL, WIN)
    mel_energy = jnp.dot(power_bins, filters, precision=lax.Precision.HIGHEST)
    log_energy = jnp.log(mel_energy + 1e-06)
    valid_mel = (jnp.arange(mel_count, dtype=jnp.int32) < length // HOP)[:, None]
    valid_count = (length // HOP).astype(jnp.float32)
    mel_mean = lax.optimization_barrier(jnp.sum(jnp.where(valid_mel, log_energy, 0.0), axis=0)) / valid_count
    second = lax.optimization_barrier(jnp.sum(jnp.where(valid_mel, log_energy * log_energy, 0.0), axis=0)) / valid_count
    mel_var = second - mel_mean * mel_mean
    normed_mel = jnp.where(valid_mel, (log_energy - mel_mean) * lax.rsqrt(mel_var + 1e-05), 0.0)
    return normed_mel.astype(jnp.bfloat16)

def encode_one(samples, length, sub_weight, value_weight, gate_weight, out_weight, depth_kernel, norm_scale, norm_shift):
    normed_mel = log_mel(samples, length)
    padded = jnp.pad(normed_mel, ((TAPS // 2, TAPS // 2), (0, 0)))
    leading = padded[:STRIDE * FRAMES].reshape(FRAMES, STRIDE * MEL)
    second = padded[STRIDE:STRIDE * FRAMES + STRIDE].reshape(FRAMES, STRIDE * MEL)[:, :(TAPS - STRIDE) * MEL]
    stacked = jnp.concatenate([leading, second], axis=1)
    features = jnp.dot(stacked, sub_weight, preferred_element_type=jnp.float32).astype(jnp.bfloat16)
    widened = features.astype(jnp.float32)
    centered = widened - lax.optimization_barrier(jnp.mean(widened, axis=1, keepdims=True))
    spread = lax.optimization_barrier(jnp.mean(centered * centered, axis=1, keepdims=True))
    normed = (centered * lax.rsqrt(spread + 1e-05)).astype(jnp.bfloat16)
    value_sum = jnp.dot(normed, value_weight, preferred_element_type=jnp.float32)
    gate_sum = jnp.dot(normed, gate_weight, preferred_element_type=jnp.float32)
    valid_frames = (jnp.arange(FRAMES, dtype=jnp.int32) < length // (STRIDE * HOP))[:, None]
    gated = jnp.where(valid_frames, value_sum * jax.nn.sigmoid(gate_sum), 0.0).astype(jnp.bfloat16)
    reach = KERNEL // 2
    padded_gated = jnp.pad(gated.astype(jnp.float32), ((reach, reach), (0, 0)))
    depthwise = jnp.zeros((FRAMES, D), jnp.float32)
    for tap_index in range(KERNEL):
        depthwise = depthwise + depth_kernel[tap_index] * padded_gated[tap_index:tap_index + FRAMES]
    shifted = depthwise * norm_scale + norm_shift
    activated = jax.nn.silu(shifted).astype(jnp.bfloat16)
    quarter = D // N_MP
    running = jnp.zeros((FRAMES, D), jnp.float32)
    for group in range(N_MP):
        partial_term = jnp.dot(activated[:, group * quarter:(group + 1) * quarter], out_weight[group * quarter:(group + 1) * quarter], preferred_element_type=jnp.float32)
        running = running + lax.optimization_barrier(partial_term.astype(jnp.bfloat16)).astype(jnp.float32)
    encoded = jnp.where(valid_frames, features.astype(jnp.float32) + running, 0.0)
    return encoded.astype(jnp.bfloat16)

def reference(waveform, lengths, sub_weight, value_weight, gate_weight, out_weight, depth_kernel, norm_scale, norm_shift):

    def utterance(inputs):
        return encode_one(inputs[0], inputs[1], sub_weight, value_weight, gate_weight, out_weight, depth_kernel, norm_scale, norm_shift)
    return lax.map(utterance, (waveform, lengths))
```

```python
import math

import jax
import jax.numpy as jnp
import numpy as np
from jax import lax
from jax.experimental import pallas as pl
from jax.experimental.pallas import tpu as pltpu
from jax.sharding import PartitionSpec as P

MEL = 128
WIN = 400
HOP = 160
STRIDE = 4
KERNEL = 31
BINS = 201
F32 = jnp.float32
BF16 = jnp.bfloat16
Z = 16
HOPS = (8, 7)
NT = (((1,), (1,)), ((), ()))


def mel_filters():
    mel_top = 2595.0 * math.log10(1.0 + 8000.0 / 700.0)
    borders = np.asarray(
        [
            700.0 * (10.0 ** (i * mel_top / (MEL + 1) / 2595.0) - 1.0) * WIN / 16000.0
            for i in range(MEL + 2)
        ],
        np.float32,
    )
    centers = np.arange(BINS, dtype=np.float32)[:, None]
    middle = borders[1:-1][None, :]
    lower = np.minimum(borders[:-2], borders[1:-1] - np.float32(1.0))[None, :]
    upper = np.maximum(borders[2:], borders[1:-1] + np.float32(1.0))[None, :]
    rising = (centers - lower) / (middle - lower)
    falling = (upper - centers) / (upper - middle)
    full = np.zeros((256, MEL), np.float32)
    full[:BINS] = np.maximum(np.float32(0.0), np.minimum(rising, falling))
    return full


def fourier_table():
    n = np.arange(WIN)
    window = 0.5 - 0.5 * np.cos(2.0 * np.pi * n / WIN)
    phases = 2.0 * np.pi * ((n[:, None] * np.arange(BINS)[None, :]) % WIN) / WIN
    full = np.zeros((512, 512), np.float32)
    full[:WIN, :BINS] = window[:, None] * np.cos(phases)
    full[:WIN, 256 : 256 + BINS] = window[:, None] * np.sin(phases)
    return full


def exact_dot(a, b):
    return jnp.dot(a, b, precision=lax.Precision.HIGHEST, preferred_element_type=F32)


def kernel(
    len_ref, wav, subw, valw, gatw, outw, dk, scale, shift, table, filters,
    out_ref,
    wbuf, halo, pack, packf, st1, compf, subr, vg, ow, subf, ma, mb, nm, fb, feats, normed,
    gp, gf, act, ps, rs,
    h_s, h_r, s1_s, s1_r, ma_s, ma_r, mb_s, mb_r, nm_s, nm_r, mh_s, mh_r, ag_s, ag_r,
    gh_s, gh_r, rs_s, rs_r, ring_s, ring_r, sib_s, sib_r,
):
    dp = lax.axis_index("dp")
    tm = lax.axis_index("tm")
    mp = lax.axis_index("mp")
    z_hi = tm // 8
    q = tm % 8
    core = tm % 2
    z = z_hi * 8 + dp
    length = len_ref[0]
    seg = tm * 4 + mp

    def remote(src, dst, ssem, rsem, **dev):
        return pltpu.make_async_remote_copy(
            src_ref=src, dst_ref=dst, send_sem=ssem, recv_sem=rsem,
            device_id=dev, device_id_type=pl.DeviceIdType.MESH,
        )

    tm_up, tm_down = (tm + 1) % 16, (tm + 15) % 16
    z_side = [(z + 1) % Z, (z + Z - 1) % Z]
    z_dev = [{"dp": s % 8, "tm": (s // 8) * 8 + q} for s in z_side]

    barrier = pltpu.get_barrier_semaphore()

    def greet(**dev):
        pl.semaphore_signal(
            barrier, inc=1, device_id=dev, device_id_type=pl.DeviceIdType.MESH
        )

    for i in range(1, 8):
        greet(tm=z_hi * 8 + (q + i) % 8)
    for dev in z_dev:
        greet(**dev)
    for i in range(4):
        if i:
            greet(mp=(mp + i) % 4)
        greet(tm=(1 - z_hi) * 8 + q, mp=(mp + i) % 4)
        greet(tm=tm_up, mp=(mp + i) % 4)
        greet(tm=tm_down, mp=(mp + i) % 4)

    packf[...] = jnp.zeros_like(packf)
    packf[0:7, :] = subw[...].astype(F32)
    packf[16:28, :] = valw[...].astype(F32)
    packf[32:44, :] = gatw[...].astype(F32)
    eye = (
        lax.broadcasted_iota(jnp.int32, (16, 12), 0)
        == lax.broadcasted_iota(jnp.int32, (16, 12), 1)
    ).astype(BF16)
    packf[48:64, :] = lax.dot_general(eye, outw[...], NT, preferred_element_type=F32)
    pack[...] = packf[...].astype(BF16)
    st1[q] = pack[...]

    pl.semaphore_wait(barrier, 7 + 2 + 3 + 4 + 8)

    prev_mp = (mp + 3) % 4
    prev_tm = (tm + 15 + (mp + 3) // 4) % 16
    halo_copy = remote(wav.at[0:8], halo, h_s, h_r, tm=prev_tm, mp=prev_mp)
    halo_copy.start()

    def stage1(i):
        return remote(
            pack, st1.at[q], s1_s.at[i], s1_r.at[i], tm=z_hi * 8 + (q + i) % 8
        )

    for i in range(1, 8):
        stage1(i).start()

    chains = {"S": (0, subr, 32), "V": (1, vg, 48), "O": (2, ow, 48)}

    def slot(chain, at, side):
        _, ref, rows = chains[chain]
        return ref.at[(at % 8) * 2 + at // 8, pl.ds(pl.multiple_of(side * rows, 16), rows)]

    def source(d, k):
        return (z + Z - k) % Z if d == 0 else (z + k) % Z

    def ring(chain, d, k):
        n = chains[chain][0]
        ref = slot(chain, source(d, k - 1), core)
        return remote(ref, ref, ring_s.at[n, d, k], ring_r.at[n, d, k], **z_dev[d])

    def ring_in(chain, d, k):
        n = chains[chain][0]
        ref = slot(chain, source(d, k), core)
        return remote(ref, ref, ring_s.at[n, d, k], ring_r.at[n, d, k], **z_dev[d])

    def sibling(chain, d, k, side):
        n = chains[chain][0]
        ref = slot(chain, source(d, k), side)
        return remote(
            ref, ref, sib_s.at[n, d, k], sib_r.at[n, d, k], tm=tm + 1 - 2 * core
        )

    def begin(chain):
        for d in range(2):
            ring(chain, d, 1).start()

    def serve(chain, first, last):
        for k in range(first, last + 1):
            for d in range(2):
                if k > HOPS[d]:
                    continue
                ring_in(chain, d, k).wait_recv()
                if k + 1 <= HOPS[d]:
                    ring(chain, d, k + 1).start()
                sibling(chain, d, k, core).start()

    def finish(chain):
        for d in range(2):
            for k in range(1, HOPS[d] + 1):
                sibling(chain, d, k, 1 - core).wait_recv()

    def drain(chain):
        for d in range(2):
            for k in range(1, HOPS[d] + 1):
                ring(chain, d, k).wait_send()
                sibling(chain, d, k, core).wait_send()

    position = (
        seg * 40960
        + lax.broadcasted_iota(jnp.int32, (328, 128), 0) * 128
        + lax.broadcasted_iota(jnp.int32, (328, 128), 1)
    )
    wbuf[0:320] = jnp.where(position[:320] < length, wav[...], 0.0)

    for i in range(1, 8):
        stage1(i).wait_recv()
    for i in range(8):
        block = st1[i].astype(F32)
        compf[7 * i : 7 * i + 7, 0:384] = block[0:7]
        for j in range(3):
            compf[64 + 12 * i : 76 + 12 * i, 384 * j : 384 * j + 384] = block[
                16 * j + 16 : 16 * j + 28
            ]
    compf[56:64, 0:384] = jnp.zeros((8, 384), F32)
    mine = (z % 8) * 2 + z // 8
    subr[mine] = compf[0:64, 0:384].astype(BF16)
    vg[mine] = compf[64:160, 0:768].astype(BF16)
    ow[mine] = compf[64:160, 768:1152].astype(BF16)
    begin("S")
    begin("V")

    halo_copy.wait_recv()
    wbuf[320:328] = jnp.where(position[320:328] < length, halo[...], 0.0)
    wide = jnp.concatenate([wbuf[pl.ds(c, 64, stride=5), :] for c in range(7)], axis=1)
    frames = jnp.concatenate(
        [wide[:, :512]]
        + [pltpu.roll(wide, 896 - HOP * j, 1)[:, :512] for j in range(1, STRIDE)],
        axis=0,
    )
    spectrum = exact_dot(frames, table[...])
    power = spectrum[:, :256] * spectrum[:, :256] + spectrum[:, 256:] * spectrum[:, 256:]
    log_energy = jnp.log(exact_dot(power, filters[...]) + 1e-06)
    row = lax.broadcasted_iota(jnp.int32, (256, MEL), 0)
    valid_mel = seg * 256 + (row % 64) * 4 + row // 64 < length // HOP
    kept = jnp.where(valid_mel, log_energy, 0.0)
    ma[q] = jnp.concatenate(
        [
            jnp.sum(kept, axis=0, keepdims=True),
            jnp.sum(kept * kept, axis=0, keepdims=True),
            jnp.zeros((6, MEL), F32),
        ],
        axis=0,
    )

    def moments_a(i):
        return remote(
            ma.at[q], ma.at[q], ma_s.at[i], ma_r.at[i], tm=z_hi * 8 + (q + i) % 8
        )

    for i in range(1, 8):
        moments_a(i).start()
    serve("S", 1, 2)
    for i in range(1, 8):
        moments_a(i).wait_recv()
    total = ma[0]
    for i in range(1, 8):
        total = total + ma[i]
    place = z_hi * 4 + mp
    mb[place] = total

    def moments_b(i):
        other = (place + i) % 8
        return remote(
            mb.at[place], mb.at[place], mb_s.at[i], mb_r.at[i],
            tm=(other // 4) * 8 + q, mp=other % 4,
        )

    for i in range(1, 8):
        moments_b(i).start()
    serve("S", 3, 4)
    serve("V", 1, 1)
    for i in range(1, 8):
        moments_b(i).wait_recv()
    total = mb[0]
    for i in range(1, 8):
        total = total + mb[i]
    count = (length // HOP).astype(F32)
    mel_mean = total[0:1] / count
    mel_var = total[1:2] / count - mel_mean * mel_mean
    normed_mel = jnp.where(
        valid_mel, (log_energy - mel_mean) * lax.rsqrt(mel_var + 1e-05), 0.0
    ).astype(BF16)
    own = pl.ds(pl.multiple_of(16 + mp * 64, 16), 64)
    for j in range(STRIDE):
        nm[j, own, :] = normed_mel[j * 64 : j * 64 + 64]

    def mel_gather(i):
        ref = nm.at[:, own, :]
        return remote(ref, ref, nm_s.at[i], nm_r.at[i], mp=(mp + i) % 4)

    def mel_gather_in(i):
        there = pl.ds(pl.multiple_of(16 + ((mp + 4 - i) % 4) * 64, 16), 64)
        ref = nm.at[:, there, :]
        return remote(ref, ref, nm_s.at[i], nm_r.at[i], mp=(mp + i) % 4)

    def mel_halo(i):
        return remote(
            nm.at[:, pl.ds(256, 16), :], nm.at[:, pl.ds(0, 16), :],
            mh_s.at[i], mh_r, tm=tm_up, mp=(mp + i) % 4,
        )

    for i in range(1, 4):
        mel_gather(i).start()

    @pl.when(mp == 3)
    def _():
        for i in range(4):
            mel_halo(i).start()

    serve("S", 5, 6)
    serve("V", 2, 2)
    serve("S", 7, 8)
    serve("V", 3, 3)
    begin("O")
    finish("S")
    for s in range(Z):
        subf[56 * s : 56 * s + 56, :] = subr[s].astype(F32)[0:56]
    for i in range(1, 4):
        mel_gather_in(i).wait_recv()
    mel_halo(0).wait_recv()

    head = subf[0:384, :].astype(BF16)
    rest = subf[384:896, :].astype(BF16)
    before = jnp.dot(
        jnp.concatenate([nm[j] for j in range(1, STRIDE)], axis=1), head,
        preferred_element_type=F32,
    )
    edge = lax.broadcasted_iota(jnp.int32, (272, 384), 0) < jnp.where(tm == 0, 16, 0)
    fb[...] = jnp.where(edge, 0.0, before)
    here = jnp.dot(
        jnp.concatenate([nm[j, 16:272] for j in range(STRIDE)], axis=1), rest,
        preferred_element_type=F32,
    )
    feats[mp] = (here + fb[15:271, :]).astype(BF16)

    def gather(i):
        return remote(
            feats.at[mp], feats.at[mp], ag_s.at[i], ag_r.at[i], mp=(mp + i) % 4
        )

    def gather_in(i):
        ref = feats.at[(mp + 4 - i) % 4]
        return remote(ref, ref, ag_s.at[i], ag_r.at[i], mp=(mp + i) % 4)

    for i in range(1, 4):
        gather(i).start()
    serve("V", 4, 5)
    serve("O", 1, 1)
    serve("V", 6, 7)
    serve("O", 2, 2)
    serve("V", 8, 8)
    serve("O", 3, 4)
    for i in range(1, 4):
        gather_in(i).wait_recv()

    @pl.loop(0, 8)
    def _(b):
        rows = pl.ds(pl.multiple_of(b * 32, 32), 32)
        wide = jnp.concatenate([feats[g, rows, :] for g in range(4)], axis=1).astype(F32)
        centered = wide - jnp.mean(wide, axis=1, keepdims=True)
        spread = jnp.mean(centered * centered, axis=1, keepdims=True)
        normed[rows, :] = (centered * lax.rsqrt(spread + 1e-05)).astype(BF16)

    finish("V")
    both = jnp.dot(
        normed[...], vg[...].reshape(1536, 768), preferred_element_type=F32
    )
    valid = (
        tm * 256 + lax.broadcasted_iota(jnp.int32, (256, 384), 0)
        < length // (STRIDE * HOP)
    )
    gated = jnp.where(valid, both[:, :384] * jax.nn.sigmoid(both[:, 384:]), 0.0)
    gp[16:272, :] = gated.astype(BF16)

    to_next = remote(
        gp.at[pl.ds(256, 16)], gp.at[pl.ds(0, 16)], gh_s.at[0], gh_r.at[0], tm=tm_up
    )
    to_prev = remote(
        gp.at[pl.ds(16, 16)], gp.at[pl.ds(272, 16)], gh_s.at[1], gh_r.at[1], tm=tm_down
    )
    to_next.start()
    to_prev.start()
    serve("O", 5, 6)
    gf[16:272, :] = gp[16:272, :].astype(F32)
    to_next.wait_recv()
    to_prev.wait_recv()
    gf[0:16, :] = jnp.where(tm == 0, 0.0, gp[0:16, :].astype(F32))
    gf[272:288, :] = jnp.where(tm == 15, 0.0, gp[272:288, :].astype(F32))

    @pl.loop(0, 12)
    def _(b):
        rows = pl.multiple_of((b // 3) * 64, 64)
        lanes = pl.ds(pl.multiple_of((b % 3) * 128, 128), 128)
        window = gf[pl.ds(rows, 96), lanes]
        taps = dk[:, lanes]
        out = jnp.zeros((64, 128), F32)
        for p in range(8):
            part = jnp.zeros((72, 128), F32)
            for w in range(4):
                tap = 8 * w + p - 1
                if tap >= 0:
                    part = part + taps[tap : tap + 1] * window[8 * w : 8 * w + 72]
            if p:
                part = pltpu.roll(part, 72 - p, 0)
            out = out + part[:64]
        moved = out * scale[:, lanes] + shift[:, lanes]
        act[pl.ds(rows, 64), lanes] = (moved * jax.nn.sigmoid(moved)).astype(BF16)

    serve("O", 7, 8)
    finish("O")

    def partial(g):
        block = ow[pl.ds(g * 4, 4)].reshape(384, 384)
        return lax.dot_general(
            act[...], block, NT, preferred_element_type=F32
        ).astype(BF16)

    def scatter(i):
        return remote(ps.at[i], rs.at[i], rs_s.at[i], rs_r.at[i], mp=(mp + i) % 4)

    for i in (2, 1, 3):
        ps[i] = partial((mp + i) % 4)
        scatter(i).start()
    summed = partial(mp).astype(F32)
    for i in range(1, 4):
        scatter(i).wait_recv()
        summed = summed + rs[i].astype(F32)
    out_ref[...] = jnp.where(valid, feats[mp].astype(F32) + summed, 0.0).astype(BF16)

    halo_copy.wait_send()
    for i in range(1, 8):
        stage1(i).wait_send()
        moments_a(i).wait_send()
        moments_b(i).wait_send()
    for i in range(1, 4):
        mel_gather(i).wait_send()
        gather(i).wait_send()
        scatter(i).wait_send()

    @pl.when(mp == 3)
    def _():
        for i in range(4):
            mel_halo(i).wait_send()

    to_next.wait_send()
    to_prev.wait_send()
    for chain in "SVO":
        drain(chain)


def shards(
    waveform, lengths, sub_weight, value_weight, gate_weight, out_weight,
    depth_kernel, norm_scale, norm_shift,
):
    vmem = pl.BlockSpec(memory_space=pltpu.VMEM)
    dma = pltpu.SemaphoreType.DMA
    encoded = pl.pallas_call(
        kernel,
        out_shape=jax.ShapeDtypeStruct((256, 384), BF16),
        in_specs=[pl.BlockSpec(memory_space=pltpu.SMEM)] + [vmem] * 10,
        out_specs=vmem,
        scratch_shapes=[
            pltpu.VMEM((328, 128), F32),
            pltpu.VMEM((8, 128), F32),
            pltpu.VMEM((64, 384), BF16),
            pltpu.VMEM((64, 384), F32),
            pltpu.VMEM((8, 64, 384), BF16),
            pltpu.VMEM((160, 1152), F32),
            pltpu.VMEM((Z, 64, 384), BF16),
            pltpu.VMEM((Z, 96, 768), BF16),
            pltpu.VMEM((Z, 96, 384), BF16),
            pltpu.VMEM((896, 384), F32),
            pltpu.VMEM((8, 8, 128), F32),
            pltpu.VMEM((8, 8, 128), F32),
            pltpu.VMEM((4, 272, 128), BF16),
            pltpu.VMEM((272, 384), F32),
            pltpu.VMEM((4, 256, 384), BF16),
            pltpu.VMEM((256, 1536), BF16),
            pltpu.VMEM((288, 384), BF16),
            pltpu.VMEM((288, 384), F32),
            pltpu.VMEM((256, 384), BF16),
            pltpu.VMEM((4, 256, 384), BF16),
            pltpu.VMEM((4, 256, 384), BF16),
            dma, dma,
            dma((8,)), dma((8,)),
            dma((8,)), dma((8,)),
            dma((8,)), dma((8,)),
            dma((4,)), dma((4,)),
            dma((4,)), dma,
            dma((4,)), dma((4,)),
            dma((2,)), dma((2,)),
            dma((4,)), dma((4,)),
            dma((3, 2, 9)), dma((3, 2, 9)),
            dma((3, 2, 9)), dma((3, 2, 9)),
        ],
        compiler_params=pltpu.CompilerParams(
            collective_id=0, has_side_effects=True, vmem_limit_bytes=48 * 1024 * 1024
        ),
    )(
        lengths,
        waveform.reshape(320, 128),
        sub_weight,
        value_weight,
        gate_weight,
        out_weight,
        depth_kernel,
        norm_scale.reshape(1, 384),
        norm_shift.reshape(1, 384),
        jnp.asarray(fourier_table()),
        jnp.asarray(mel_filters()),
    )
    return encoded[None]


def solution(mesh):
    placed = (
        P("dp", ("tm", "mp")),
        P("dp"),
        P(("dp", "tm"), "mp"),
        P(("dp", "tm"), "mp"),
        P(("dp", "tm"), "mp"),
        P("mp", ("dp", "tm")),
        P(None, "mp"),
        P("mp"),
        P("mp"),
    )
    return jax.shard_map(
        shards, mesh=mesh, in_specs=placed, out_specs=P("dp", "tm", "mp"), check_vma=False
    )
```

```python
import math

import jax
import jax.numpy as jnp
import numpy as np
from jax import lax
from jax.experimental import pallas as pl
from jax.experimental.pallas import tpu as pltpu
from jax.sharding import PartitionSpec as P

MEL = 128
WIN = 400
HOP = 160
STRIDE = 4
KERNEL = 31
BINS = 201
F32 = jnp.float32
BF16 = jnp.bfloat16
Z = 16
NT = (((1,), (1,)), ((), ()))


def mel_filters():
    mel_top = 2595.0 * math.log10(1.0 + 8000.0 / 700.0)
    borders = np.asarray(
        [
            700.0 * (10.0 ** (i * mel_top / (MEL + 1) / 2595.0) - 1.0) * WIN / 16000.0
            for i in range(MEL + 2)
        ],
        np.float32,
    )
    centers = np.arange(BINS, dtype=np.float32)[:, None]
    middle = borders[1:-1][None, :]
    lower = np.minimum(borders[:-2], borders[1:-1] - np.float32(1.0))[None, :]
    upper = np.maximum(borders[2:], borders[1:-1] + np.float32(1.0))[None, :]
    rising = (centers - lower) / (middle - lower)
    falling = (upper - centers) / (upper - middle)
    full = np.zeros((256, MEL), np.float32)
    full[:BINS] = np.maximum(np.float32(0.0), np.minimum(rising, falling))
    return full


def fourier_table():
    n = np.arange(WIN)
    window = 0.5 - 0.5 * np.cos(2.0 * np.pi * n / WIN)
    phases = 2.0 * np.pi * ((n[:, None] * np.arange(BINS)[None, :]) % WIN) / WIN
    full = np.zeros((512, 512), np.float32)
    full[:WIN, :BINS] = window[:, None] * np.cos(phases)
    full[:WIN, 256 : 256 + BINS] = window[:, None] * np.sin(phases)
    return full


def exact_dot(a, b):
    return jnp.dot(a, b, precision=lax.Precision.HIGHEST, preferred_element_type=F32)


def kernel(
    len_ref, subw, valw, gatw, outw, wav_hbm, dk_hbm, scale, shift, table_hbm, filters_hbm,
    out_ref,
    wav, dk, table, filters, wbuf, halo, pack, packf, got, own48, w, sf, vw, gw, ow,
    ma, mb, le, nmf, feats, normed, gp, gf, act, ps, rs,
    in_s, h_s, h_r, c_s, c_r, ma_s, ma_r, mb_s, mb_r, le_s, le_r, lh_s, lh_r, ag_s, ag_r,
    gh_s, gh_r, rs_s, rs_r, z_s, z_r, x_s, x_r, sib_s, sib_r,
):
    dp = lax.axis_index("dp")
    tm = lax.axis_index("tm")
    mp = lax.axis_index("mp")
    z_hi = tm // 8
    q = tm % 8
    x = q // 2
    core = tm % 2
    z = z_hi * 8 + dp
    slab = dp * 2 + z_hi
    length = len_ref[0]
    seg = tm * 4 + mp
    tm_up, tm_down = (tm + 1) % 16, (tm + 15) % 16
    twin = tm + 1 - 2 * core

    def remote(src, dst, ssem, rsem, **dev):
        return pltpu.make_async_remote_copy(
            src_ref=src, dst_ref=dst, send_sem=ssem, recv_sem=rsem,
            device_id=dev, device_id_type=pl.DeviceIdType.MESH,
        )

    loads = [
        pltpu.make_async_copy(there, here, in_s.at[i])
        for i, (there, here) in enumerate(
            [(wav_hbm, wav), (table_hbm, table), (filters_hbm, filters), (dk_hbm, dk)]
        )
    ]
    for load in loads:
        load.start()

    barrier = pltpu.get_barrier_semaphore()

    def greet(**dev):
        pl.semaphore_signal(
            barrier, inc=1, device_id=dev, device_id_type=pl.DeviceIdType.MESH
        )

    def along_z(i):
        other = (z + i) % Z
        return {"dp": other % 8, "tm": (other // 8) * 8 + q}

    for i in range(1, Z):
        greet(**along_z(i))
    for i in range(1, 8):
        greet(tm=z_hi * 8 + (q + i) % 8)
    for i in range(4):
        if i:
            greet(mp=(mp + i) % 4)
            greet(tm=(1 - z_hi) * 8 + q, mp=(mp + i) % 4)
        greet(tm=tm_up, mp=(mp + i) % 4)
        greet(tm=tm_down, mp=(mp + i) % 4)

    packf[...] = jnp.zeros_like(packf)
    packf[0, 0:7, :] = subw[...].astype(F32)
    packf[0, 7:19, :] = outw[...].astype(F32)
    packf[1, 0:12, :] = valw[...].astype(F32)
    packf[1, 12:24, :] = gatw[...].astype(F32)
    pack[...] = packf[...].astype(BF16)

    pl.semaphore_wait(barrier, 15 + 7 + 3 + 3 + 8)

    swap = remote(pack.at[1 - core], got, c_s, c_r, tm=twin)
    swap.start()
    loads[0].wait()
    prev_mp = (mp + 3) % 4
    prev_tm = (tm + 15 + (mp + 3) // 4) % 16
    halo_copy = remote(wav.at[0:8], halo, h_s, h_r, tm=prev_tm, mp=prev_mp)
    halo_copy.start()

    position = (
        seg * 40960
        + lax.broadcasted_iota(jnp.int32, (328, 128), 0) * 128
        + lax.broadcasted_iota(jnp.int32, (328, 128), 1)
    )
    wbuf[0:320] = jnp.where(position[:320] < length, wav[...], 0.0)

    swap.wait_recv()
    mine, other = packf[core], got[...].astype(F32)
    first = jnp.where(core == 0, mine, other)
    second = jnp.where(core == 0, other, mine)

    @pl.when(core == 0)
    def _():
        own48[0:7] = first[0:7]
        own48[7:14] = second[0:7]
        own48[14:16] = jnp.zeros((2, 384), F32)
        own48[16:28] = first[7:19]
        own48[28:40] = second[7:19]
        own48[40:48] = jnp.zeros((8, 384), F32)

    @pl.when(core == 1)
    def _():
        own48[0:12] = first[0:12]
        own48[12:24] = second[0:12]
        own48[24:36] = first[12:24]
        own48[36:48] = second[12:24]

    batch = [core * 3 + j for j in range(3)]
    for j in range(3):
        w[batch[j], slab, x] = own48[16 * j : 16 * j + 16].astype(BF16)

    def push_z(j, i):
        ref = w.at[batch[j], slab, x]
        return remote(ref, ref, z_s.at[j, i], z_r.at[j, i], **along_z(i))

    def from_z(j, i):
        at = (z + Z - i) % Z
        ref = w.at[batch[j], (at % 8) * 2 + at // 8, x]
        return remote(ref, ref, z_s.at[j, i], z_r.at[j, i], **along_z(i))

    def push_x(j, i):
        ref = w.at[batch[j], :, x]
        return remote(
            ref, ref, x_s.at[j, i], x_r.at[j, i],
            tm=z_hi * 8 + ((x + i) % 4) * 2 + core,
        )

    def from_x(j, i):
        ref = w.at[batch[j], :, (x + 4 - i) % 4]
        return remote(
            ref, ref, x_s.at[j, i], x_r.at[j, i],
            tm=z_hi * 8 + ((x + i) % 4) * 2 + core,
        )

    def push_twin(j):
        ref = w.at[batch[j]]
        return remote(ref, ref, sib_s.at[j], sib_r.at[j], tm=twin)

    def from_twin(j):
        ref = w.at[(1 - core) * 3 + j]
        return remote(ref, ref, sib_s.at[j], sib_r.at[j], tm=twin)

    def send_z(j):
        for i in (8, 7, 9, 6, 10, 5, 11, 4, 12, 3, 13, 2, 14, 1, 15):
            push_z(j, i).start()

    def send_x(j):
        for i in range(1, Z):
            from_z(j, i).wait_recv()
        for i in (2, 1, 3):
            push_x(j, i).start()

    def send_twin(j):
        for i in range(1, 4):
            from_x(j, i).wait_recv()
        push_twin(j).start()

    send_z(0)

    halo_copy.wait_recv()
    wbuf[320:328] = jnp.where(position[320:328] < length, halo[...], 0.0)
    wide = jnp.concatenate([wbuf[pl.ds(c, 64, stride=5), :] for c in range(7)], axis=1)
    frames = jnp.concatenate(
        [wide[:, :512]]
        + [pltpu.roll(wide, 896 - HOP * j, 1)[:, :512] for j in range(1, STRIDE)],
        axis=0,
    )
    loads[1].wait()
    loads[2].wait()
    spectrum = exact_dot(frames, table[...])
    power = spectrum[:, :256] * spectrum[:, :256] + spectrum[:, 256:] * spectrum[:, 256:]
    log_energy = jnp.log(exact_dot(power, filters[...]) + 1e-06)
    row = lax.broadcasted_iota(jnp.int32, (256, MEL), 0)
    valid_mel = seg * 256 + (row % 64) * 4 + row // 64 < length // HOP
    kept = jnp.where(valid_mel, log_energy, 0.0)
    ma[q] = jnp.concatenate(
        [
            jnp.sum(kept, axis=0, keepdims=True),
            jnp.sum(kept * kept, axis=0, keepdims=True),
            jnp.zeros((6, MEL), F32),
        ],
        axis=0,
    )

    def moments_a(i):
        return remote(
            ma.at[q], ma.at[q], ma_s.at[i], ma_r.at[i], tm=z_hi * 8 + (q + i) % 8
        )

    for i in range(1, 8):
        moments_a(i).start()

    own = pl.ds(pl.multiple_of(8 + mp * 64, 8), 64)
    for j in range(STRIDE):
        le[j, own, :] = log_energy[j * 64 : j * 64 + 64]

    def mel_gather(i):
        ref = le.at[:, own, :]
        return remote(ref, ref, le_s.at[i], le_r.at[i], mp=(mp + i) % 4)

    def mel_gather_in(i):
        there = pl.ds(pl.multiple_of(8 + ((mp + 4 - i) % 4) * 64, 8), 64)
        ref = le.at[:, there, :]
        return remote(ref, ref, le_s.at[i], le_r.at[i], mp=(mp + i) % 4)

    def mel_halo(i):
        return remote(
            le.at[:, pl.ds(256, 8), :], le.at[:, pl.ds(0, 8), :],
            lh_s.at[i], lh_r, tm=tm_up, mp=(mp + i) % 4,
        )

    @pl.when(mp == 3)
    def _():
        for i in range(4):
            mel_halo(i).start()

    for i in (2, 1, 3):
        mel_gather(i).start()
    for i in range(1, 8):
        moments_a(i).wait_recv()
    total = ma[0]
    for i in range(1, 8):
        total = total + ma[i]
    place = z_hi * 4 + mp
    mb[place] = total

    def moments_b(i):
        away = (place + i) % 8
        return remote(
            mb.at[place], mb.at[place], mb_s.at[i], mb_r.at[i],
            tm=(away // 4) * 8 + q, mp=away % 4,
        )

    for i in (4, 5, 6, 7, 3, 2, 1):
        moments_b(i).start()
    send_z(1)
    send_x(0)
    send_z(2)
    for i in range(1, 8):
        moments_b(i).wait_recv()
    total = mb[0]
    for i in range(1, 8):
        total = total + mb[i]
    count = (length // HOP).astype(F32)
    mel_mean = total[0:1] / count
    mel_var = total[1:2] / count - mel_mean * mel_mean
    mel_scale = lax.rsqrt(mel_var + 1e-05)
    for i in range(1, 4):
        mel_gather_in(i).wait_recv()
    mel_halo(0).wait_recv()
    time = tm * 256 - 8 + lax.broadcasted_iota(jnp.int32, (264, MEL), 0)
    for j in range(STRIDE):
        known = (time >= 0) & (time * 4 + j < length // HOP)
        nmf[j] = jnp.where(known, (le[j] - mel_mean) * mel_scale, 0.0)

    send_x(1)
    send_twin(0)
    from_twin(0).wait_recv()

    for s in range(Z):
        for i in range(4):
            sf[56 * s + 14 * i : 56 * s + 14 * i + 14, :] = w[0, s, i].astype(F32)[0:14]
    stacked = jnp.concatenate(
        [nmf[j, 7:263] for j in range(1, STRIDE)] + [nmf[j, 8:264] for j in range(STRIDE)],
        axis=1,
    ).astype(BF16)
    feats[mp] = jnp.dot(
        stacked, sf[...].astype(BF16), preferred_element_type=F32
    ).astype(BF16)

    def gather(i):
        return remote(
            feats.at[mp], feats.at[mp], ag_s.at[i], ag_r.at[i], mp=(mp + i) % 4
        )

    def gather_in(i):
        ref = feats.at[(mp + 4 - i) % 4]
        return remote(ref, ref, ag_s.at[i], ag_r.at[i], mp=(mp + i) % 4)

    for i in (2, 1, 3):
        gather(i).start()
    send_x(2)
    send_twin(1)
    send_twin(2)

    for i in range(1, 4):
        gather_in(i).wait_recv()

    @pl.loop(0, 8)
    def _(b):
        rows = pl.ds(pl.multiple_of(b * 32, 32), 32)
        wide = jnp.concatenate([feats[g, rows, :] for g in range(4)], axis=1).astype(F32)
        centered = wide - jnp.mean(wide, axis=1, keepdims=True)
        spread = jnp.mean(centered * centered, axis=1, keepdims=True)
        normed[rows, :] = (centered * lax.rsqrt(spread + 1e-05)).astype(BF16)

    from_twin(1).wait_recv()
    from_twin(2).wait_recv()

    @pl.loop(0, Z)
    def _(s):
        value, gate = [], []
        for i in range(4):
            top, middle, bottom = (w[b, s, i].astype(F32) for b in (3, 4, 5))
            value += [top, middle[0:8]]
            gate += [middle[8:16], bottom]
        vw[s] = jnp.concatenate(value, axis=0).astype(BF16)
        gw[s] = jnp.concatenate(gate, axis=0).astype(BF16)

    value_sum = jnp.dot(
        normed[...], vw[...].reshape(1536, 384), preferred_element_type=F32
    )
    gate_sum = jnp.dot(
        normed[...], gw[...].reshape(1536, 384), preferred_element_type=F32
    )
    valid = (
        tm * 256 + lax.broadcasted_iota(jnp.int32, (256, 384), 0)
        < length // (STRIDE * HOP)
    )
    gated = jnp.where(valid, value_sum * jax.nn.sigmoid(gate_sum), 0.0)
    gp[16:272, :] = gated.astype(BF16)

    to_next = remote(
        gp.at[pl.ds(256, 16)], gp.at[pl.ds(0, 16)], gh_s.at[0], gh_r.at[0], tm=tm_up
    )
    to_prev = remote(
        gp.at[pl.ds(16, 16)], gp.at[pl.ds(272, 16)], gh_s.at[1], gh_r.at[1], tm=tm_down
    )
    to_next.start()
    to_prev.start()
    gf[16:272, :] = gp[16:272, :].astype(F32)
    loads[3].wait()

    def depthwise(block, column):
        rows = pl.multiple_of(block * 64, 64)
        lanes = pl.ds(pl.multiple_of(column * 128, 128), 128)
        window = gf[pl.ds(rows, 96), lanes]
        taps = dk[:, lanes]
        out = jnp.zeros((64, 128), F32)
        for p in range(8):
            part = jnp.zeros((72, 128), F32)
            for k in range(4):
                tap = 8 * k + p - 1
                if tap >= 0:
                    part = part + taps[tap : tap + 1] * window[8 * k : 8 * k + 72]
            if p:
                part = pltpu.roll(part, 72 - p, 0)
            out = out + part[:64]
        moved = out * scale[lanes].reshape(1, 128) + shift[lanes].reshape(1, 128)
        act[pl.ds(rows, 64), lanes] = (moved * jax.nn.sigmoid(moved)).astype(BF16)

    @pl.loop(0, 6)
    def _(b):
        depthwise(b // 3 + 1, b % 3)

    to_next.wait_recv()
    to_prev.wait_recv()
    gf[0:16, :] = jnp.where(tm == 0, 0.0, gp[0:16, :].astype(F32))
    gf[272:288, :] = jnp.where(tm == 15, 0.0, gp[272:288, :].astype(F32))

    @pl.loop(0, 6)
    def _(b):
        depthwise((b // 3) * 3, b % 3)

    @pl.loop(0, Z)
    def _(s):
        rows = []
        for i in range(4):
            rows += [w[1, s, i].astype(F32), w[2, s, i].astype(F32)[0:8]]
        ow[s] = jnp.concatenate(rows, axis=0).astype(BF16)

    def partial(g):
        block = ow[pl.ds(g * 4, 4)].reshape(384, 384)
        return lax.dot_general(
            act[...], block, NT, preferred_element_type=F32
        ).astype(BF16)

    def scatter(i):
        return remote(ps.at[i], rs.at[i], rs_s.at[i], rs_r.at[i], mp=(mp + i) % 4)

    for i in (2, 1, 3):
        ps[i] = partial((mp + i) % 4)
        scatter(i).start()
    summed = partial(mp).astype(F32)
    for i in range(1, 4):
        scatter(i).wait_recv()
        summed = summed + rs[i].astype(F32)
    out_ref[...] = jnp.where(valid, feats[mp].astype(F32) + summed, 0.0).astype(BF16)

    halo_copy.wait_send()
    swap.wait_send()
    for i in range(1, 8):
        moments_a(i).wait_send()
        moments_b(i).wait_send()
    for i in range(1, 4):
        mel_gather(i).wait_send()
        gather(i).wait_send()
        scatter(i).wait_send()

    @pl.when(mp == 3)
    def _():
        for i in range(4):
            mel_halo(i).wait_send()

    to_next.wait_send()
    to_prev.wait_send()
    for j in range(3):
        for i in range(1, Z):
            push_z(j, i).wait_send()
        for i in range(1, 4):
            push_x(j, i).wait_send()
        push_twin(j).wait_send()


def shards(
    waveform, lengths, sub_weight, value_weight, gate_weight, out_weight,
    depth_kernel, norm_scale, norm_shift,
):
    vmem = pl.BlockSpec(memory_space=pltpu.VMEM)
    hbm = pl.BlockSpec(memory_space=pltpu.HBM)
    dma = pltpu.SemaphoreType.DMA
    encoded = pl.pallas_call(
        kernel,
        out_shape=jax.ShapeDtypeStruct((256, 384), BF16),
        in_specs=[pl.BlockSpec(memory_space=pltpu.SMEM)] + [vmem] * 4 + [hbm] * 2 + [vmem] * 2 + [hbm] * 2,
        out_specs=vmem,
        scratch_shapes=[
            pltpu.VMEM((320, 128), F32),
            pltpu.VMEM((KERNEL, 384), F32),
            pltpu.VMEM((512, 512), F32),
            pltpu.VMEM((256, MEL), F32),
            pltpu.VMEM((328, 128), F32),
            pltpu.VMEM((8, 128), F32),
            pltpu.VMEM((2, 32, 384), BF16),
            pltpu.VMEM((2, 32, 384), F32),
            pltpu.VMEM((32, 384), BF16),
            pltpu.VMEM((48, 384), F32),
            pltpu.VMEM((6, Z, 4, 16, 384), BF16),
            pltpu.VMEM((896, 384), F32),
            pltpu.VMEM((Z, 96, 384), BF16),
            pltpu.VMEM((Z, 96, 384), BF16),
            pltpu.VMEM((Z, 96, 384), BF16),
            pltpu.VMEM((8, 8, 128), F32),
            pltpu.VMEM((8, 8, 128), F32),
            pltpu.VMEM((4, 264, 128), F32),
            pltpu.VMEM((4, 264, 128), F32),
            pltpu.VMEM((4, 256, 384), BF16),
            pltpu.VMEM((256, 1536), BF16),
            pltpu.VMEM((288, 384), BF16),
            pltpu.VMEM((288, 384), F32),
            pltpu.VMEM((256, 384), BF16),
            pltpu.VMEM((4, 256, 384), BF16),
            pltpu.VMEM((4, 256, 384), BF16),
            dma((4,)),
            dma, dma,
            dma, dma,
            dma((8,)), dma((8,)),
            dma((8,)), dma((8,)),
            dma((4,)), dma((4,)),
            dma((4,)), dma,
            dma((4,)), dma((4,)),
            dma((2,)), dma((2,)),
            dma((4,)), dma((4,)),
            dma((3, Z)), dma((3, Z)),
            dma((3, 4)), dma((3, 4)),
            dma((3,)), dma((3,)),
        ],
        compiler_params=pltpu.CompilerParams(
            collective_id=0, has_side_effects=True, vmem_limit_bytes=60 * 1024 * 1024
        ),
    )(
        lengths,
        sub_weight,
        value_weight,
        gate_weight,
        out_weight.T,
        waveform.reshape(320, 128),
        depth_kernel,
        norm_scale,
        norm_shift,
        jnp.asarray(fourier_table()),
        jnp.asarray(mel_filters()),
    )
    return encoded[None]


def solution(mesh):
    placed = (
        P("dp", ("tm", "mp")),
        P("dp"),
        P(("dp", "tm"), "mp"),
        P(("dp", "tm"), "mp"),
        P(("dp", "tm"), "mp"),
        P("mp", ("dp", "tm")),
        P(None, "mp"),
        P("mp"),
        P("mp"),
    )
    return jax.shard_map(
        shards, mesh=mesh, in_specs=placed, out_specs=P("dp", "tm", "mp"), check_vma=False
    )
```

```python
import math

import jax
import jax.numpy as jnp
import numpy as np
from jax import lax
from jax.experimental import pallas as pl
from jax.experimental.pallas import tpu as pltpu
from jax.sharding import PartitionSpec as P

MEL = 128
WIN = 400
HOP = 160
STRIDE = 4
KERNEL = 31
BINS = 201
F32 = jnp.float32
BF16 = jnp.bfloat16
Z = 16
NT = (((1,), (1,)), ((), ()))


def mel_filters():
    mel_top = 2595.0 * math.log10(1.0 + 8000.0 / 700.0)
    borders = np.asarray(
        [
            700.0 * (10.0 ** (i * mel_top / (MEL + 1) / 2595.0) - 1.0) * WIN / 16000.0
            for i in range(MEL + 2)
        ],
        np.float32,
    )
    centers = np.arange(BINS, dtype=np.float32)[:, None]
    middle = borders[1:-1][None, :]
    lower = np.minimum(borders[:-2], borders[1:-1] - np.float32(1.0))[None, :]
    upper = np.maximum(borders[2:], borders[1:-1] + np.float32(1.0))[None, :]
    rising = (centers - lower) / (middle - lower)
    falling = (upper - centers) / (upper - middle)
    full = np.zeros((256, MEL), np.float32)
    full[:BINS] = np.maximum(np.float32(0.0), np.minimum(rising, falling))
    return full


def fourier_table():
    n = np.arange(WIN)
    window = 0.5 - 0.5 * np.cos(2.0 * np.pi * n / WIN)
    phases = 2.0 * np.pi * ((n[:, None] * np.arange(BINS)[None, :]) % WIN) / WIN
    full = np.zeros((512, 512), np.float32)
    full[:WIN, :BINS] = window[:, None] * np.cos(phases)
    full[:WIN, 256 : 256 + BINS] = window[:, None] * np.sin(phases)
    return full


def exact_dot(a, b):
    return jnp.dot(a, b, precision=lax.Precision.HIGHEST, preferred_element_type=F32)


def kernel(
    len_ref, subw, valw, gatw, outw, wav_hbm, dk_hbm, scale, shift, table_hbm, filters_hbm,
    out_ref,
    wav, dk, table, filters, wbuf, halo, lg, pack, packf, got, own48, w, sf, vw, gw, ow,
    ma, mb, le, nmf, feats, normed, gp, gf, act, ps, rs,
    in_s, h_s, h_r, c_s, c_r, ma_s, ma_r, mb_s, mb_r, le_s, le_r, lh_s, lh_r, ag_s, ag_r,
    gh_s, gh_r, rs_s, rs_r, z_s, z_r, x_s, x_r, sib_s, sib_r,
):
    dp = lax.axis_index("dp")
    tm = lax.axis_index("tm")
    mp = lax.axis_index("mp")
    z_hi = tm // 8
    q = tm % 8
    x = q // 2
    core = tm % 2
    z = z_hi * 8 + dp
    length = len_ref[0]
    seg = tm * 4 + mp
    tm_up, tm_down = (tm + 1) % 16, (tm + 15) % 16
    twin = tm + 1 - 2 * core

    def remote(src, dst, ssem, rsem, **dev):
        return pltpu.make_async_remote_copy(
            src_ref=src, dst_ref=dst, send_sem=ssem, recv_sem=rsem,
            device_id=dev, device_id_type=pl.DeviceIdType.MESH,
        )

    loads = [
        pltpu.make_async_copy(there, here, in_s.at[i])
        for i, (there, here) in enumerate(
            [(wav_hbm, wav), (table_hbm, table), (filters_hbm, filters), (dk_hbm, dk)]
        )
    ]
    for load in loads:
        load.start()

    barrier = pltpu.get_barrier_semaphore()

    def greet(**dev):
        pl.semaphore_signal(
            barrier, inc=1, device_id=dev, device_id_type=pl.DeviceIdType.MESH
        )

    def along_z(i):
        other = (z + i) % Z
        return {"dp": other % 8, "tm": (other // 8) * 8 + q}

    for i in range(1, Z):
        greet(**along_z(i))
    for i in range(1, 8):
        greet(tm=z_hi * 8 + (q + i) % 8)
    for i in range(4):
        if i:
            greet(mp=(mp + i) % 4)
            greet(tm=(1 - z_hi) * 8 + q, mp=(mp + i) % 4)
        greet(tm=tm_up, mp=(mp + i) % 4)
        greet(tm=tm_down, mp=(mp + i) % 4)

    packf[...] = jnp.zeros_like(packf)
    packf[0, 0:7, :] = subw[...].astype(F32)
    packf[0, 7:19, :] = outw[...].astype(F32)
    packf[1, 0:12, :] = valw[...].astype(F32)
    packf[1, 12:24, :] = gatw[...].astype(F32)
    pack[...] = packf[...].astype(BF16)

    position = (
        seg * 40960
        + lax.broadcasted_iota(jnp.int32, (328, 128), 0) * 128
        + lax.broadcasted_iota(jnp.int32, (328, 128), 1)
    )

    def log_mel(start, count, steps):
        wide = jnp.concatenate(
            [wbuf[pl.ds(5 * start + c, count, stride=5), :] for c in range(7)], axis=1
        )
        frames = jnp.concatenate(
            [
                (pltpu.roll(wide, 896 - HOP * j, 1) if j else wide)[:, :512]
                for j in steps
            ],
            axis=0,
        )
        spectrum = exact_dot(frames, table[...])
        power = (
            spectrum[:, :256] * spectrum[:, :256] + spectrum[:, 256:] * spectrum[:, 256:]
        )
        energy = jnp.log(exact_dot(power, filters[...]) + 1e-06)
        for k, j in enumerate(steps):
            lg[j, start : start + count, :] = energy[k * count : k * count + count]

    loads[0].wait()
    wbuf[0:320] = jnp.where(position[:320] < length, wav[...], 0.0)
    wbuf[320:328] = jnp.zeros((8, 128), F32)
    loads[1].wait()
    loads[2].wait()
    log_mel(0, 64, range(STRIDE))

    pl.semaphore_wait(barrier, 15 + 7 + 3 + 3 + 8)

    swap = remote(pack.at[1 - core], got, c_s, c_r, tm=twin)
    swap.start()
    prev_mp = (mp + 3) % 4
    prev_tm = (tm + 15 + (mp + 3) // 4) % 16
    halo_copy = remote(wav.at[0:8], halo, h_s, h_r, tm=prev_tm, mp=prev_mp)
    halo_copy.start()

    swap.wait_recv()
    mine, other = packf[core], got[...].astype(F32)
    first = jnp.where(core == 0, mine, other)
    second = jnp.where(core == 0, other, mine)

    @pl.when(core == 0)
    def _():
        own48[0:7] = first[0:7]
        own48[7:14] = second[0:7]
        own48[14:16] = jnp.zeros((2, 384), F32)
        own48[16:28] = first[7:19]
        own48[28:40] = second[7:19]
        own48[40:48] = jnp.zeros((8, 384), F32)

    @pl.when(core == 1)
    def _():
        own48[0:12] = first[0:12]
        own48[12:24] = second[0:12]
        own48[24:36] = first[12:24]
        own48[36:48] = second[12:24]

    def on(which):
        return pl.when(core == which)

    for c in range(2):
        @on(c)
        def _(c=c):
            for j in range(3):
                w[3 * c + j, z % 4, z // 4, x] = own48[16 * j : 16 * j + 16].astype(BF16)

    def push_z(b, i):
        ref = w.at[b, z % 4, z // 4, x]
        return remote(ref, ref, z_s.at[b, i], z_r.at[b, i], **along_z(i))

    def from_z(b, i):
        at = (z + Z - i) % Z
        ref = w.at[b, at % 4, at // 4, x]
        return remote(ref, ref, z_s.at[b, i], z_r.at[b, i], **along_z(i))

    near = {1: pl.ds(0, 4), 15: pl.ds(0, 4), 2: pl.ds(0, 2), 14: pl.ds(2, 2)}

    def push_near(b, i):
        ref = w.at[b, z % 4, near[i], x]
        return remote(ref, ref, z_s.at[b, i], z_r.at[b, i], **along_z(i))

    def from_near(b, i):
        ref = w.at[b, (z + Z - i) % 4, near[i], x]
        return remote(ref, ref, z_s.at[b, i], z_r.at[b, i], **along_z(i))

    def column(b, i):
        return w.at[b, :, :, (x + 4 - i) % 4]

    def push_x(b, i):
        return remote(
            column(b, 0), column(b, 0), x_s.at[b, i], x_r.at[b, i],
            tm=z_hi * 8 + ((x + i) % 4) * 2 + core,
        )

    def from_x(b, i):
        return remote(
            column(b, i), column(b, i), x_s.at[b, i], x_r.at[b, i],
            tm=z_hi * 8 + ((x + i) % 4) * 2 + core,
        )

    def twin_copy(b, i):
        return remote(column(b, i), column(b, i), sib_s.at[b, i], sib_r.at[b, i], tm=twin)

    FAR = (8, 4, 12)
    AHEAD = (8, 7, 9, 6, 10, 5, 11, 4, 12, 3, 13, 2, 14, 1, 15)

    def send_far(b):
        for i in FAR:
            push_z(b, i).start()

    def send_near(b):
        for i in FAR:
            from_z(b, i).wait_recv()
        for i in near:
            push_near(b, i).start()

    def send_x(b):
        for i in near if b else range(1, Z):
            (from_near if b else from_z)(b, i).wait_recv()
        for i in (2, 1, 3):
            push_x(b, i).start()
        twin_copy(b, 0).start()

    def send_twin(b):
        for i in (1, 3, 2):
            from_x(b, i).wait_recv()
            twin_copy(b, i).start()

    def from_twin(b):
        for i in (0, 1, 3, 2):
            twin_copy(b, i).wait_recv()

    @on(0)
    def _():
        for i in AHEAD:
            push_z(0, i).start()

    @on(1)
    def _():
        send_far(3)

    halo_copy.wait_recv()
    wbuf[320:328] = jnp.where(position[320:328] < length, halo[...], 0.0)
    log_mel(56, 8, (2, 3))
    row = lax.broadcasted_iota(jnp.int32, (256, MEL), 0)
    valid_mel = seg * 256 + (row % 64) * 4 + row // 64 < length // HOP
    log_energy = jnp.concatenate([lg[j] for j in range(STRIDE)], axis=0)
    kept = jnp.where(valid_mel, log_energy, 0.0)
    ma[q] = jnp.concatenate(
        [
            jnp.sum(kept, axis=0, keepdims=True),
            jnp.sum(kept * kept, axis=0, keepdims=True),
            jnp.zeros((6, MEL), F32),
        ],
        axis=0,
    )

    def moments_a(i):
        return remote(
            ma.at[q], ma.at[q], ma_s.at[i], ma_r.at[i], tm=z_hi * 8 + (q + i) % 8
        )

    for i in range(1, 8):
        moments_a(i).start()

    own = pl.ds(pl.multiple_of(8 + mp * 64, 8), 64)
    for j in range(STRIDE):
        le[j, own, :] = log_energy[j * 64 : j * 64 + 64]

    def mel_gather(i):
        ref = le.at[:, own, :]
        return remote(ref, ref, le_s.at[i], le_r.at[i], mp=(mp + i) % 4)

    def mel_gather_in(i):
        there = pl.ds(pl.multiple_of(8 + ((mp + 4 - i) % 4) * 64, 8), 64)
        ref = le.at[:, there, :]
        return remote(ref, ref, le_s.at[i], le_r.at[i], mp=(mp + i) % 4)

    def mel_halo(i):
        return remote(
            le.at[:, pl.ds(256, 8), :], le.at[:, pl.ds(0, 8), :],
            lh_s.at[i], lh_r, tm=tm_up, mp=(mp + i) % 4,
        )

    @pl.when(mp == 3)
    def _():
        for i in range(4):
            mel_halo(i).start()

    for i in (2, 1, 3):
        mel_gather(i).start()

    @on(1)
    def _():
        send_near(3)

    for i in range(1, 8):
        moments_a(i).wait_recv()
    total = ma[0]
    for i in range(1, 8):
        total = total + ma[i]
    place = z_hi * 4 + mp
    mb[place] = total

    def moments_b(i):
        away = (place + i) % 8
        return remote(
            mb.at[place], mb.at[place], mb_s.at[i], mb_r.at[i],
            tm=(away // 4) * 8 + q, mp=away % 4,
        )

    for i in (4, 5, 6, 7, 3, 2, 1):
        moments_b(i).start()

    @on(0)
    def _():
        send_x(0)

    @on(1)
    def _():
        send_far(4)
        send_far(5)

    for i in range(1, 8):
        moments_b(i).wait_recv()
    total = mb[0]
    for i in range(1, 8):
        total = total + mb[i]
    count = (length // HOP).astype(F32)
    mel_mean = total[0:1] / count
    mel_var = total[1:2] / count - mel_mean * mel_mean
    mel_scale = lax.rsqrt(mel_var + 1e-05)
    for i in range(1, 4):
        mel_gather_in(i).wait_recv()
    mel_halo(0).wait_recv()
    time = tm * 256 - 8 + lax.broadcasted_iota(jnp.int32, (264, MEL), 0)
    for j in range(STRIDE):
        known = (time >= 0) & (time * 4 + j < length // HOP)
        nmf[j] = jnp.where(known, (le[j] - mel_mean) * mel_scale, 0.0)

    @on(0)
    def _():
        send_twin(0)
        send_far(1)
        send_far(2)

    @on(1)
    def _():
        send_x(3)
        send_near(4)
        send_near(5)
        from_twin(0)

    for s in range(Z):
        for i in range(4):
            at = (s % 2) * 8 + s // 2
            sf[56 * s + 14 * i : 56 * s + 14 * i + 14, :] = w[0, at % 4, at // 4, i].astype(
                F32
            )[0:14]
    stacked = jnp.concatenate(
        [nmf[j, 7:263] for j in range(1, STRIDE)] + [nmf[j, 8:264] for j in range(STRIDE)],
        axis=1,
    ).astype(BF16)
    feats[mp] = jnp.dot(
        stacked, sf[...].astype(BF16), preferred_element_type=F32
    ).astype(BF16)

    def gather(i):
        return remote(
            feats.at[mp], feats.at[mp], ag_s.at[i], ag_r.at[i], mp=(mp + i) % 4
        )

    def gather_in(i):
        ref = feats.at[(mp + 4 - i) % 4]
        return remote(ref, ref, ag_s.at[i], ag_r.at[i], mp=(mp + i) % 4)

    for i in (2, 1, 3):
        gather(i).start()

    @on(0)
    def _():
        send_near(1)
        send_near(2)
        send_x(1)
        send_x(2)

    @on(1)
    def _():
        send_x(4)
        send_x(5)
        for b in (3, 4, 5):
            send_twin(b)

    for i in range(1, 4):
        gather_in(i).wait_recv()

    @pl.loop(0, 8)
    def _(b):
        rows = pl.ds(pl.multiple_of(b * 32, 32), 32)
        wide = jnp.concatenate([feats[g, rows, :] for g in range(4)], axis=1).astype(F32)
        centered = wide - jnp.mean(wide, axis=1, keepdims=True)
        spread = jnp.mean(centered * centered, axis=1, keepdims=True)
        normed[rows, :] = (centered * lax.rsqrt(spread + 1e-05)).astype(BF16)

    @on(0)
    def _():
        for b in (3, 4, 5):
            from_twin(b)

    @pl.loop(0, Z)
    def _(s):
        value, gate = [], []
        at = (s % 2) * 8 + s // 2
        for i in range(4):
            top, middle, bottom = (
                w[b, at % 4, at // 4, i].astype(F32) for b in (3, 4, 5)
            )
            value += [top, middle[0:8]]
            gate += [middle[8:16], bottom]
        vw[s] = jnp.concatenate(value, axis=0).astype(BF16)
        gw[s] = jnp.concatenate(gate, axis=0).astype(BF16)

    value_sum = jnp.dot(
        normed[...], vw[...].reshape(1536, 384), preferred_element_type=F32
    )
    gate_sum = jnp.dot(
        normed[...], gw[...].reshape(1536, 384), preferred_element_type=F32
    )
    valid = (
        tm * 256 + lax.broadcasted_iota(jnp.int32, (256, 384), 0)
        < length // (STRIDE * HOP)
    )
    gated = jnp.where(valid, value_sum * jax.nn.sigmoid(gate_sum), 0.0)
    gp[16:272, :] = gated.astype(BF16)

    to_next = remote(
        gp.at[pl.ds(256, 16)], gp.at[pl.ds(0, 16)], gh_s.at[0], gh_r.at[0], tm=tm_up
    )
    to_prev = remote(
        gp.at[pl.ds(16, 16)], gp.at[pl.ds(272, 16)], gh_s.at[1], gh_r.at[1], tm=tm_down
    )
    to_next.start()
    to_prev.start()
    gf[16:272, :] = gp[16:272, :].astype(F32)
    loads[3].wait()

    def depthwise(block, column):
        rows = pl.multiple_of(block * 64, 64)
        lanes = pl.ds(pl.multiple_of(column * 128, 128), 128)
        window = gf[pl.ds(rows, 96), lanes]
        taps = dk[:, lanes]
        out = jnp.zeros((64, 128), F32)
        for p in range(8):
            part = jnp.zeros((72, 128), F32)
            for k in range(4):
                tap = 8 * k + p - 1
                if tap >= 0:
                    part = part + taps[tap : tap + 1] * window[8 * k : 8 * k + 72]
            if p:
                part = pltpu.roll(part, 72 - p, 0)
            out = out + part[:64]
        moved = out * scale[lanes].reshape(1, 128) + shift[lanes].reshape(1, 128)
        act[pl.ds(rows, 64), lanes] = (moved * jax.nn.sigmoid(moved)).astype(BF16)

    @pl.loop(0, 6)
    def _(b):
        depthwise(b // 3 + 1, b % 3)

    to_next.wait_recv()
    to_prev.wait_recv()
    gf[0:16, :] = jnp.where(tm == 0, 0.0, gp[0:16, :].astype(F32))
    gf[272:288, :] = jnp.where(tm == 15, 0.0, gp[272:288, :].astype(F32))

    @pl.loop(0, 6)
    def _(b):
        depthwise((b // 3) * 3, b % 3)

    @on(0)
    def _():
        send_twin(1)
        send_twin(2)

    @on(1)
    def _():
        from_twin(1)
        from_twin(2)

    @pl.loop(0, Z)
    def _(s):
        rows = []
        at = (s % 2) * 8 + s // 2
        for i in range(4):
            rows += [
                w[1, at % 4, at // 4, i].astype(F32),
                w[2, at % 4, at // 4, i].astype(F32)[0:8],
            ]
        ow[s] = jnp.concatenate(rows, axis=0).astype(BF16)

    def partial(g):
        block = ow[pl.ds(g * 4, 4)].reshape(384, 384)
        return lax.dot_general(
            act[...], block, NT, preferred_element_type=F32
        ).astype(BF16)

    def scatter(i):
        return remote(ps.at[i], rs.at[i], rs_s.at[i], rs_r.at[i], mp=(mp + i) % 4)

    for i in (2, 1, 3):
        ps[i] = partial((mp + i) % 4)
        scatter(i).start()
    summed = partial(mp).astype(F32)
    for i in range(1, 4):
        scatter(i).wait_recv()
        summed = summed + rs[i].astype(F32)
    out_ref[...] = jnp.where(valid, feats[mp].astype(F32) + summed, 0.0).astype(BF16)

    halo_copy.wait_send()
    swap.wait_send()
    for i in range(1, 8):
        moments_a(i).wait_send()
        moments_b(i).wait_send()
    for i in range(1, 4):
        mel_gather(i).wait_send()
        gather(i).wait_send()
        scatter(i).wait_send()

    @pl.when(mp == 3)
    def _():
        for i in range(4):
            mel_halo(i).wait_send()

    to_next.wait_send()
    to_prev.wait_send()

    for c in range(2):
        @on(c)
        def _(c=c):
            for b in range(3 * c, 3 * c + 3):
                for i in FAR if b else AHEAD:
                    push_z(b, i).wait_send()
                for i in near if b else ():
                    push_near(b, i).wait_send()
                for i in range(1, 4):
                    push_x(b, i).wait_send()
                for i in range(4):
                    twin_copy(b, i).wait_send()


def shards(
    waveform, lengths, sub_weight, value_weight, gate_weight, out_weight,
    depth_kernel, norm_scale, norm_shift,
):
    vmem = pl.BlockSpec(memory_space=pltpu.VMEM)
    hbm = pl.BlockSpec(memory_space=pltpu.HBM)
    dma = pltpu.SemaphoreType.DMA
    encoded = pl.pallas_call(
        kernel,
        out_shape=jax.ShapeDtypeStruct((256, 384), BF16),
        in_specs=[pl.BlockSpec(memory_space=pltpu.SMEM)] + [vmem] * 4 + [hbm] * 2 + [vmem] * 2 + [hbm] * 2,
        out_specs=vmem,
        scratch_shapes=[
            pltpu.VMEM((320, 128), F32),
            pltpu.VMEM((KERNEL, 384), F32),
            pltpu.VMEM((512, 512), F32),
            pltpu.VMEM((256, MEL), F32),
            pltpu.VMEM((328, 128), F32),
            pltpu.VMEM((8, 128), F32),
            pltpu.VMEM((4, 64, 128), F32),
            pltpu.VMEM((2, 32, 384), BF16),
            pltpu.VMEM((2, 32, 384), F32),
            pltpu.VMEM((32, 384), BF16),
            pltpu.VMEM((48, 384), F32),
            pltpu.VMEM((6, 4, 4, 4, 16, 384), BF16),
            pltpu.VMEM((896, 384), F32),
            pltpu.VMEM((Z, 96, 384), BF16),
            pltpu.VMEM((Z, 96, 384), BF16),
            pltpu.VMEM((Z, 96, 384), BF16),
            pltpu.VMEM((8, 8, 128), F32),
            pltpu.VMEM((8, 8, 128), F32),
            pltpu.VMEM((4, 264, 128), F32),
            pltpu.VMEM((4, 264, 128), F32),
            pltpu.VMEM((4, 256, 384), BF16),
            pltpu.VMEM((256, 1536), BF16),
            pltpu.VMEM((288, 384), BF16),
            pltpu.VMEM((288, 384), F32),
            pltpu.VMEM((256, 384), BF16),
            pltpu.VMEM((4, 256, 384), BF16),
            pltpu.VMEM((4, 256, 384), BF16),
            dma((4,)),
            dma, dma,
            dma, dma,
            dma((8,)), dma((8,)),
            dma((8,)), dma((8,)),
            dma((4,)), dma((4,)),
            dma((4,)), dma,
            dma((4,)), dma((4,)),
            dma((2,)), dma((2,)),
            dma((4,)), dma((4,)),
            dma((6, Z)), dma((6, Z)),
            dma((6, 4)), dma((6, 4)),
            dma((6, 4)), dma((6, 4)),
        ],
        compiler_params=pltpu.CompilerParams(
            collective_id=0, has_side_effects=True, vmem_limit_bytes=60 * 1024 * 1024
        ),
    )(
        lengths,
        sub_weight,
        value_weight,
        gate_weight,
        out_weight.T,
        waveform.reshape(320, 128),
        depth_kernel,
        norm_scale,
        norm_shift,
        jnp.asarray(fourier_table()),
        jnp.asarray(mel_filters()),
    )
    return encoded[None]


def solution(mesh):
    placed = (
        P("dp", ("tm", "mp")),
        P("dp"),
        P(("dp", "tm"), "mp"),
        P(("dp", "tm"), "mp"),
        P(("dp", "tm"), "mp"),
        P("mp", ("dp", "tm")),
        P(None, "mp"),
        P("mp"),
        P("mp"),
    )
    return jax.shard_map(
        shards, mesh=mesh, in_specs=placed, out_specs=P("dp", "tm", "mp"), check_vma=False
    )
```

```python
import math

import jax
import jax.numpy as jnp
import numpy as np
from jax import lax
from jax.experimental import pallas as pl
from jax.experimental.pallas import tpu as pltpu
from jax.sharding import PartitionSpec as P

MEL = 128
WIN = 400
HOP = 160
STRIDE = 4
KERNEL = 31
BINS = 201
F32 = jnp.float32
BF16 = jnp.bfloat16
Z = 16
NT = (((1,), (1,)), ((), ()))


def mel_filters():
    mel_top = 2595.0 * math.log10(1.0 + 8000.0 / 700.0)
    borders = np.asarray(
        [
            700.0 * (10.0 ** (i * mel_top / (MEL + 1) / 2595.0) - 1.0) * WIN / 16000.0
            for i in range(MEL + 2)
        ],
        np.float32,
    )
    centers = np.arange(BINS, dtype=np.float32)[:, None]
    middle = borders[1:-1][None, :]
    lower = np.minimum(borders[:-2], borders[1:-1] - np.float32(1.0))[None, :]
    upper = np.maximum(borders[2:], borders[1:-1] + np.float32(1.0))[None, :]
    rising = (centers - lower) / (middle - lower)
    falling = (upper - centers) / (upper - middle)
    full = np.zeros((256, MEL), np.float32)
    full[:BINS] = np.maximum(np.float32(0.0), np.minimum(rising, falling))
    return full


def fourier_table():
    n = np.arange(WIN)
    window = 0.5 - 0.5 * np.cos(2.0 * np.pi * n / WIN)
    phases = 2.0 * np.pi * ((n[:, None] * np.arange(BINS)[None, :]) % WIN) / WIN
    full = np.zeros((512, 512), np.float32)
    full[:WIN, :BINS] = window[:, None] * np.cos(phases)
    full[:WIN, 256 : 256 + BINS] = window[:, None] * np.sin(phases)
    return full


def exact_dot(a, b):
    return jnp.dot(a, b, precision=lax.Precision.HIGHEST, preferred_element_type=F32)


def kernel(
    len_ref, subw, valw, gatw, outw, wav_hbm, dk_hbm, scale, shift, table_hbm, filters_hbm,
    out_ref,
    wav, dk, table, filters, wbuf, halo, lg, pack, packf, got, own48, w, sf, vw, gw, ow,
    ma, mb, le, nmf, feats, normed, gp, gf, act, ps, rs,
    in_s, h_s, h_r, c_s, c_r, ma_s, ma_r, mb_s, mb_r, le_s, le_r, lh_s, lh_r, ag_s, ag_r,
    gh_s, gh_r, rs_s, rs_r, z_s, far_r, near_r, x_s, x_r, sib_s, sib_r,
):
    dp = lax.axis_index("dp")
    tm = lax.axis_index("tm")
    mp = lax.axis_index("mp")
    z_hi = tm // 8
    q = tm % 8
    x = q // 2
    core = tm % 2
    z = z_hi * 8 + dp
    length = len_ref[0]
    seg = tm * 4 + mp
    tm_up, tm_down = (tm + 1) % 16, (tm + 15) % 16
    twin = tm + 1 - 2 * core

    def remote(src, dst, ssem, rsem, **dev):
        return pltpu.make_async_remote_copy(
            src_ref=src, dst_ref=dst, send_sem=ssem, recv_sem=rsem,
            device_id=dev, device_id_type=pl.DeviceIdType.MESH,
        )

    def arrived(ref, rsem):
        remote(ref, ref, c_s, rsem, tm=twin).wait_recv()

    def left(ref, ssem):
        remote(ref, ref, ssem, c_r, tm=twin).wait_send()

    loads = [
        pltpu.make_async_copy(there, here, in_s.at[i])
        for i, (there, here) in enumerate(
            [(wav_hbm, wav), (table_hbm, table), (filters_hbm, filters), (dk_hbm, dk)]
        )
    ]
    for load in loads:
        load.start()

    barrier = pltpu.get_barrier_semaphore()

    def greet(**dev):
        pl.semaphore_signal(
            barrier, inc=1, device_id=dev, device_id_type=pl.DeviceIdType.MESH
        )

    def along_z(i):
        other = (z + i) % Z
        return {"dp": other % 8, "tm": (other // 8) * 8 + q}

    for i in range(1, Z):
        greet(**along_z(i))
    for i in range(1, 8):
        greet(tm=z_hi * 8 + (q + i) % 8)
    for i in range(4):
        if i:
            greet(mp=(mp + i) % 4)
            greet(tm=(1 - z_hi) * 8 + q, mp=(mp + i) % 4)
        greet(tm=tm_up, mp=(mp + i) % 4)
        greet(tm=tm_down, mp=(mp + i) % 4)

    packf[...] = jnp.zeros_like(packf)
    packf[0, 0:7, :] = subw[...].astype(F32)
    packf[0, 7:19, :] = outw[...].astype(F32)
    packf[1, 0:12, :] = valw[...].astype(F32)
    packf[1, 12:24, :] = gatw[...].astype(F32)
    pack[...] = packf[...].astype(BF16)

    position = (
        seg * 40960
        + lax.broadcasted_iota(jnp.int32, (328, 128), 0) * 128
        + lax.broadcasted_iota(jnp.int32, (328, 128), 1)
    )

    def log_mel(start, count, steps):
        wide = jnp.concatenate(
            [wbuf[pl.ds(5 * start + c, count, stride=5), :] for c in range(7)], axis=1
        )
        frames = jnp.concatenate(
            [
                (pltpu.roll(wide, 896 - HOP * j, 1) if j else wide)[:, :512]
                for j in steps
            ],
            axis=0,
        )
        spectrum = exact_dot(frames, table[...])
        power = (
            spectrum[:, :256] * spectrum[:, :256] + spectrum[:, 256:] * spectrum[:, 256:]
        )
        energy = jnp.log(exact_dot(power, filters[...]) + 1e-06)
        for k, j in enumerate(steps):
            lg[j, start : start + count, :] = energy[k * count : k * count + count]

    loads[0].wait()
    wbuf[0:320] = jnp.where(position[:320] < length, wav[...], 0.0)
    wbuf[320:328] = jnp.zeros((8, 128), F32)
    loads[1].wait()
    loads[2].wait()
    log_mel(0, 64, range(STRIDE))

    pl.semaphore_wait(barrier, 15 + 7 + 3 + 3 + 8)

    swap = remote(pack.at[1 - core], got, c_s, c_r, tm=twin)
    swap.start()
    prev_mp = (mp + 3) % 4
    prev_tm = (tm + 15 + (mp + 3) // 4) % 16
    halo_copy = remote(wav.at[0:8], halo, h_s, h_r, tm=prev_tm, mp=prev_mp)
    halo_copy.start()

    swap.wait_recv()
    mine, other = packf[core], got[...].astype(F32)
    first = jnp.where(core == 0, mine, other)
    second = jnp.where(core == 0, other, mine)

    @pl.when(core == 0)
    def _():
        own48[0:7] = first[0:7]
        own48[7:14] = second[0:7]
        own48[14:16] = jnp.zeros((2, 384), F32)
        own48[16:28] = first[7:19]
        own48[28:40] = second[7:19]
        own48[40:48] = jnp.zeros((8, 384), F32)

    @pl.when(core == 1)
    def _():
        own48[0:12] = first[0:12]
        own48[12:24] = second[0:12]
        own48[24:36] = first[12:24]
        own48[36:48] = second[12:24]

    def on(which):
        return pl.when(core == which)

    for c in range(2):
        @on(c)
        def _(c=c):
            for j in range(3):
                w[3 * c + j, z % 4, z // 4, x] = own48[16 * j : 16 * j + 16].astype(BF16)

    def push(ref, ssem, rsem, **dev):
        remote(ref, ref, ssem, rsem, **dev).start()

    FAR = (8, 4, 12)
    AHEAD = (8, 7, 9, 6, 10, 5, 11, 4, 12, 3, 13, 2, 14, 1, 15)
    NEAR = {1: pl.ds(0, 4), 15: pl.ds(0, 4), 2: pl.ds(0, 2), 14: pl.ds(2, 2)}

    def own_tile(b):
        return w.at[b, z % 4, z // 4] if b == 2 else w.at[b, z % 4, z // 4, x]

    def own_class(b, part):
        return w.at[b, z % 4, part] if b == 2 else w.at[b, z % 4, part, x]

    def tiles(b, n):
        if n == 15:
            return vw.at[pl.ds(0, 15), pl.ds(0, 16)]
        if n == 3:
            return w.at[b, 0, 0, pl.ds(0, 3)]
        if n == 12:
            return w.at[b, 0, pl.ds(0, 3)]
        return w.at[b, pl.ds(0, n // 16)]

    def along_x(i):
        return {"tm": z_hi * 8 + ((x + i) % 4) * 2 + core}

    def send_far(b):
        for i in FAR if b else AHEAD:
            push(own_tile(b), z_s.at[b], far_r.at[b], **along_z(i))

    def send_near(b):
        arrived(tiles(b, 12 if b == 2 else 3), far_r.at[b])
        for i, part in NEAR.items():
            push(own_class(b, part), z_s.at[6 if b == 2 else b], near_r.at[b], **along_z(i))

    def column(b, i):
        return w.at[b, :, :, (x + 4 - i) % 4]

    def send_x(b):
        if b:
            arrived(tiles(b, 12), near_r.at[b])
        else:
            arrived(tiles(b, 15), far_r.at[b])
        for i in (2, 1, 3):
            push(column(b, 0), x_s.at[b], x_r.at[b], **along_x(i))
        push(column(b, 0), sib_s.at[b], sib_r.at[b], tm=twin)

    def send_twin(b):
        arrived(tiles(b, 48), x_r.at[b])
        for i in (1, 3, 2):
            push(column(b, i), sib_s.at[b], sib_r.at[b], tm=twin)

    def first_x():
        ref = w.at[2, z % 4, z // 4, x]
        for i in (2, 1, 3):
            push(ref, x_s.at[2], x_r.at[2], **along_x(i))

    def far_2():
        arrived(tiles(2, 3), x_r.at[2])
        send_far(2)

    def twin_2():
        arrived(tiles(2, 48), near_r.at[2])
        push(w.at[2], sib_s.at[2], sib_r.at[2], tm=twin)

    def from_twin(b):
        arrived(w.at[b], sib_r.at[b])

    halo_copy.wait_recv()
    wbuf[320:328] = jnp.where(position[320:328] < length, halo[...], 0.0)
    log_mel(56, 8, (2, 3))
    row = lax.broadcasted_iota(jnp.int32, (256, MEL), 0)
    valid_mel = seg * 256 + (row % 64) * 4 + row // 64 < length // HOP
    log_energy = jnp.concatenate([lg[j] for j in range(STRIDE)], axis=0)
    kept = jnp.where(valid_mel, log_energy, 0.0)
    place = z_hi * 4 + mp
    ma[place] = jnp.concatenate(
        [
            jnp.sum(kept, axis=0, keepdims=True),
            jnp.sum(kept * kept, axis=0, keepdims=True),
            jnp.zeros((6, MEL), F32),
        ],
        axis=0,
    )

    for i in (4, 5, 6, 7, 3, 2, 1):
        away = (place + i) % 8
        push(ma.at[place], ma_s, ma_r, tm=(away // 4) * 8 + q, mp=away % 4)

    @on(0)
    def _():
        send_far(0)
        first_x()

    @on(1)
    def _():
        send_far(3)
        send_far(4)
        send_far(5)

    own = pl.ds(pl.multiple_of(8 + mp * 64, 8), 64)
    for j in range(STRIDE):
        le[j, own, :] = log_energy[j * 64 : j * 64 + 64]

    ours = le.at[:, own, :]
    next_halo = le.at[:, pl.ds(256, 8), :], le.at[:, pl.ds(0, 8), :]

    @pl.when(mp == 3)
    def _():
        for i in range(4):
            remote(*next_halo, lh_s, lh_r, tm=tm_up, mp=(mp + i) % 4).start()

    for i in (2, 1, 3):
        push(ours, le_s, le_r, mp=(mp + i) % 4)
    arrived(ma.at[pl.ds(0, 7)], ma_r)
    total = ma[0]
    for i in range(1, 8):
        total = total + ma[i]
    mb[q] = total
    for i in range(1, 8):
        push(mb.at[q], mb_s, mb_r, tm=z_hi * 8 + (q + i) % 8)

    @on(0)
    def _():
        send_x(0)
        send_far(1)
        far_2()

    @on(1)
    def _():
        send_near(3)
        send_near(4)
        send_near(5)

    arrived(mb.at[pl.ds(0, 7)], mb_r)
    total = mb[0]
    for i in range(1, 8):
        total = total + mb[i]
    count = (length // HOP).astype(F32)
    mel_mean = total[0:1] / count
    mel_var = total[1:2] / count - mel_mean * mel_mean
    mel_scale = lax.rsqrt(mel_var + 1e-05)
    arrived(le.at[:, pl.ds(0, 192), :], le_r)
    arrived(le.at[:, pl.ds(0, 8), :], lh_r)
    time = tm * 256 - 8 + lax.broadcasted_iota(jnp.int32, (264, MEL), 0)
    for j in range(STRIDE):
        known = (time >= 0) & (time * 4 + j < length // HOP)
        nmf[j] = jnp.where(known, (le[j] - mel_mean) * mel_scale, 0.0)

    @on(0)
    def _():
        send_twin(0)

    @on(1)
    def _():
        send_x(3)
        send_x(4)
        send_x(5)
        from_twin(0)

    for s in range(Z):
        for i in range(4):
            at = (s % 2) * 8 + s // 2
            sf[56 * s + 14 * i : 56 * s + 14 * i + 14, :] = w[0, at % 4, at // 4, i].astype(
                F32
            )[0:14]
    stacked = jnp.concatenate(
        [nmf[j, 7:263] for j in range(1, STRIDE)] + [nmf[j, 8:264] for j in range(STRIDE)],
        axis=1,
    ).astype(BF16)
    feats[mp] = jnp.dot(
        stacked, sf[...].astype(BF16), preferred_element_type=F32
    ).astype(BF16)

    for i in (2, 1, 3):
        push(feats.at[mp], ag_s, ag_r, mp=(mp + i) % 4)

    @on(0)
    def _():
        send_near(1)
        send_near(2)
        send_x(1)

    @on(1)
    def _():
        for b in (3, 4, 5):
            send_twin(b)

    arrived(feats.at[pl.ds(0, 3)], ag_r)

    @pl.loop(0, 8)
    def _(b):
        rows = pl.ds(pl.multiple_of(b * 32, 32), 32)
        wide = jnp.concatenate([feats[g, rows, :] for g in range(4)], axis=1).astype(F32)
        centered = wide - jnp.mean(wide, axis=1, keepdims=True)
        spread = jnp.mean(centered * centered, axis=1, keepdims=True)
        normed[rows, :] = (centered * lax.rsqrt(spread + 1e-05)).astype(BF16)

    @on(0)
    def _():
        for b in (3, 4, 5):
            from_twin(b)

    @pl.loop(0, Z)
    def _(s):
        value, gate = [], []
        at = (s % 2) * 8 + s // 2
        for i in range(4):
            top, middle, bottom = (
                w[b, at % 4, at // 4, i].astype(F32) for b in (3, 4, 5)
            )
            value += [top, middle[0:8]]
            gate += [middle[8:16], bottom]
        vw[s] = jnp.concatenate(value, axis=0).astype(BF16)
        gw[s] = jnp.concatenate(gate, axis=0).astype(BF16)

    value_sum = jnp.dot(
        normed[...], vw[...].reshape(1536, 384), preferred_element_type=F32
    )
    gate_sum = jnp.dot(
        normed[...], gw[...].reshape(1536, 384), preferred_element_type=F32
    )
    valid = (
        tm * 256 + lax.broadcasted_iota(jnp.int32, (256, 384), 0)
        < length // (STRIDE * HOP)
    )
    gated = jnp.where(valid, value_sum * jax.nn.sigmoid(gate_sum), 0.0)
    gp[16:272, :] = gated.astype(BF16)

    to_next = remote(
        gp.at[pl.ds(256, 16)], gp.at[pl.ds(0, 16)], gh_s.at[0], gh_r.at[0], tm=tm_up
    )
    to_prev = remote(
        gp.at[pl.ds(16, 16)], gp.at[pl.ds(272, 16)], gh_s.at[1], gh_r.at[1], tm=tm_down
    )
    to_next.start()
    to_prev.start()
    gf[16:272, :] = gp[16:272, :].astype(F32)
    loads[3].wait()

    def depthwise(block, column):
        rows = pl.multiple_of(block * 64, 64)
        lanes = pl.ds(pl.multiple_of(column * 128, 128), 128)
        window = gf[pl.ds(rows, 96), lanes]
        taps = dk[:, lanes]
        out = jnp.zeros((64, 128), F32)
        for p in range(8):
            part = jnp.zeros((72, 128), F32)
            for k in range(4):
                tap = 8 * k + p - 1
                if tap >= 0:
                    part = part + taps[tap : tap + 1] * window[8 * k : 8 * k + 72]
            if p:
                part = pltpu.roll(part, 72 - p, 0)
            out = out + part[:64]
        moved = out * scale[lanes].reshape(1, 128) + shift[lanes].reshape(1, 128)
        act[pl.ds(rows, 64), lanes] = (moved * jax.nn.sigmoid(moved)).astype(BF16)

    @pl.loop(0, 6)
    def _(b):
        depthwise(b // 3 + 1, b % 3)

    @on(0)
    def _():
        twin_2()
        send_twin(1)

    @on(1)
    def _():
        from_twin(2)
        from_twin(1)

    @pl.loop(0, Z)
    def _(s):
        rows = []
        at = (s % 2) * 8 + s // 2
        for i in range(4):
            rows += [
                w[1, at % 4, at // 4, i].astype(F32),
                w[2, at % 4, at // 4, i].astype(F32)[0:8],
            ]
        ow[s] = jnp.concatenate(rows, axis=0).astype(BF16)

    def partial(rows, g):
        block = ow[pl.ds(g * 4, 4)].reshape(384, 384)
        return lax.dot_general(
            rows, block, NT, preferred_element_type=F32
        ).astype(BF16)

    def scatter(i, start, rows):
        part = pl.ds(start, rows)
        remote(
            ps.at[i, part], rs.at[i, part], rs_s, rs_r, mp=(mp + i) % 4
        ).start()

    inner = act[64:192, :]
    for i in (2, 1, 3):
        ps[i, 64:192] = partial(inner, (mp + i) % 4)
        scatter(i, 64, 128)

    to_next.wait_recv()
    to_prev.wait_recv()
    gf[0:16, :] = jnp.where(tm == 0, 0.0, gp[0:16, :].astype(F32))
    gf[272:288, :] = jnp.where(tm == 15, 0.0, gp[272:288, :].astype(F32))

    @pl.loop(0, 6)
    def _(b):
        depthwise((b // 3) * 3, b % 3)

    outer = jnp.concatenate([act[0:64, :], act[192:256, :]], axis=0)
    for i in (2, 1, 3):
        part = partial(outer, (mp + i) % 4)
        ps[i, 0:64] = part[0:64]
        ps[i, 192:256] = part[64:128]
        scatter(i, 0, 64)
        scatter(i, 192, 64)
    summed = partial(act[...], mp).astype(F32)
    arrived(rs.at[pl.ds(1, 3)], rs_r)
    for i in range(1, 4):
        summed = summed + rs[i].astype(F32)
    out_ref[...] = jnp.where(valid, feats[mp].astype(F32) + summed, 0.0).astype(BF16)

    halo_copy.wait_send()
    swap.wait_send()
    left(ma.at[pl.ds(0, 7)], ma_s)
    left(mb.at[pl.ds(0, 7)], mb_s)
    left(le.at[:, pl.ds(0, 192), :], le_s)
    left(feats.at[pl.ds(0, 3)], ag_s)
    left(rs.at[pl.ds(1, 3)], rs_s)

    @pl.when(mp == 3)
    def _():
        left(le.at[:, pl.ds(0, 32), :], lh_s)

    to_next.wait_send()
    to_prev.wait_send()

    for c in range(2):
        @on(c)
        def _(c=c):
            for b in range(3 * c, 3 * c + 3):
                if b == 2:
                    left(tiles(b, 12), z_s.at[b])
                    left(tiles(b, 48), z_s.at[6])
                    left(tiles(b, 3), x_s.at[b])
                else:
                    left(tiles(b, 15), z_s.at[b])
                    left(tiles(b, 48), x_s.at[b])
                left(w.at[b], sib_s.at[b])


def shards(
    waveform, lengths, sub_weight, value_weight, gate_weight, out_weight,
    depth_kernel, norm_scale, norm_shift,
):
    vmem = pl.BlockSpec(memory_space=pltpu.VMEM)
    hbm = pl.BlockSpec(memory_space=pltpu.HBM)
    dma = pltpu.SemaphoreType.DMA
    encoded = pl.pallas_call(
        kernel,
        out_shape=pltpu.VMEM((256, 384), BF16),
        in_specs=[pl.BlockSpec(memory_space=pltpu.SMEM)] + [vmem] * 4 + [hbm] * 2 + [vmem] * 2 + [hbm] * 2,
        out_specs=vmem,
        scratch_shapes=[
            pltpu.VMEM((320, 128), F32),
            pltpu.VMEM((KERNEL, 384), F32),
            pltpu.VMEM((512, 512), F32),
            pltpu.VMEM((256, MEL), F32),
            pltpu.VMEM((328, 128), F32),
            pltpu.VMEM((8, 128), F32),
            pltpu.VMEM((4, 64, 128), F32),
            pltpu.VMEM((2, 32, 384), BF16),
            pltpu.VMEM((2, 32, 384), F32),
            pltpu.VMEM((32, 384), BF16),
            pltpu.VMEM((48, 384), F32),
            pltpu.VMEM((6, 4, 4, 4, 16, 384), BF16),
            pltpu.VMEM((896, 384), F32),
            pltpu.VMEM((Z, 96, 384), BF16),
            pltpu.VMEM((Z, 96, 384), BF16),
            pltpu.VMEM((Z, 96, 384), BF16),
            pltpu.VMEM((8, 8, 128), F32),
            pltpu.VMEM((8, 8, 128), F32),
            pltpu.VMEM((4, 264, 128), F32),
            pltpu.VMEM((4, 264, 128), F32),
            pltpu.VMEM((4, 256, 384), BF16),
            pltpu.VMEM((256, 1536), BF16),
            pltpu.VMEM((288, 384), BF16),
            pltpu.VMEM((288, 384), F32),
            pltpu.VMEM((256, 384), BF16),
            pltpu.VMEM((4, 256, 384), BF16),
            pltpu.VMEM((4, 256, 384), BF16),
            dma((4,)),
            dma, dma,
            dma, dma,
            dma, dma,
            dma, dma,
            dma, dma,
            dma, dma,
            dma, dma,
            dma((2,)), dma((2,)),
            dma, dma,
            dma((7,)), dma((6,)), dma((6,)),
            dma((6,)), dma((6,)),
            dma((6,)), dma((6,)),
        ],
        compiler_params=pltpu.CompilerParams(
            collective_id=0, has_side_effects=True, vmem_limit_bytes=60 * 1024 * 1024
        ),
    )(
        lengths,
        sub_weight,
        value_weight,
        gate_weight,
        out_weight.T,
        waveform.reshape(320, 128),
        depth_kernel,
        norm_scale,
        norm_shift,
        jnp.asarray(fourier_table()),
        jnp.asarray(mel_filters()),
    )
    return encoded[None]


def solution(mesh):
    placed = (
        P("dp", ("tm", "mp")),
        P("dp"),
        P(("dp", "tm"), "mp"),
        P(("dp", "tm"), "mp"),
        P(("dp", "tm"), "mp"),
        P("mp", ("dp", "tm")),
        P(None, "mp"),
        P("mp"),
        P("mp"),
    )
    return jax.shard_map(
        shards, mesh=mesh, in_specs=placed, out_specs=P("dp", "tm", "mp"), check_vma=False
    )
```

```python
import math

import jax
import jax.numpy as jnp
import numpy as np
from jax import lax
from jax.experimental import pallas as pl
from jax.experimental.pallas import tpu as pltpu
from jax.sharding import PartitionSpec as P

MEL = 128
WIN = 400
HOP = 160
STRIDE = 4
KERNEL = 31
BINS = 201
F32 = jnp.float32
BF16 = jnp.bfloat16
Z = 16
NT = (((1,), (1,)), ((), ()))


def mel_filters():
    mel_top = 2595.0 * math.log10(1.0 + 8000.0 / 700.0)
    borders = np.asarray(
        [
            700.0 * (10.0 ** (i * mel_top / (MEL + 1) / 2595.0) - 1.0) * WIN / 16000.0
            for i in range(MEL + 2)
        ],
        np.float32,
    )
    centers = np.arange(BINS, dtype=np.float32)[:, None]
    middle = borders[1:-1][None, :]
    lower = np.minimum(borders[:-2], borders[1:-1] - np.float32(1.0))[None, :]
    upper = np.maximum(borders[2:], borders[1:-1] + np.float32(1.0))[None, :]
    rising = (centers - lower) / (middle - lower)
    falling = (upper - centers) / (upper - middle)
    full = np.zeros((256, MEL), np.float32)
    full[:BINS] = np.maximum(np.float32(0.0), np.minimum(rising, falling))
    return full


def fourier_table():
    n = np.arange(WIN)
    window = 0.5 - 0.5 * np.cos(2.0 * np.pi * n / WIN)
    phases = 2.0 * np.pi * ((n[:, None] * np.arange(BINS)[None, :]) % WIN) / WIN
    full = np.zeros((512, 512), np.float32)
    full[:WIN, :BINS] = window[:, None] * np.cos(phases)
    full[:WIN, 256 : 256 + BINS] = window[:, None] * np.sin(phases)
    return full


def exact_dot(a, b):
    return jnp.dot(a, b, precision=lax.Precision.HIGHEST, preferred_element_type=F32)


def kernel(
    len_ref, subw, valw, gatw, outw, wav_hbm, dk_hbm, scale, shift, table_hbm, filters_hbm,
    out_ref,
    wav, dk, table, filters, wbuf, halo, lg, pack, packf, got, own48, w, sf, vw, gw, ow,
    ma, mb, le, nmf, feats, normed, gp, gf, act, ps, rs,
    in_s, h_s, h_r, c_s, c_r, ma_s, ma_r, mb_s, mb_r, le_s, le_r, lh_s, lh_r, ag_s, ag_r,
    gh_s, gh_r, rs_s, rs_r, z_s, far_r, near_r, x_s, x_r, sib_s, sib_r,
):
    dp = lax.axis_index("dp")
    tm = lax.axis_index("tm")
    mp = lax.axis_index("mp")
    z_hi = tm // 8
    q = tm % 8
    x = q // 2
    core = tm % 2
    z = z_hi * 8 + dp
    length = len_ref[0]
    seg = tm * 4 + mp
    tm_up, tm_down = (tm + 1) % 16, (tm + 15) % 16
    twin = tm + 1 - 2 * core

    def remote(src, dst, ssem, rsem, **dev):
        return pltpu.make_async_remote_copy(
            src_ref=src, dst_ref=dst, send_sem=ssem, recv_sem=rsem,
            device_id=dev, device_id_type=pl.DeviceIdType.MESH,
        )

    def arrived(ref, rsem):
        remote(ref, ref, c_s, rsem, tm=twin).wait_recv()

    def left(ref, ssem):
        remote(ref, ref, ssem, c_r, tm=twin).wait_send()

    loads = [
        pltpu.make_async_copy(there, here, in_s.at[i])
        for i, (there, here) in enumerate(
            [(wav_hbm, wav), (table_hbm, table), (filters_hbm, filters), (dk_hbm, dk)]
        )
    ]
    for load in loads:
        load.start()

    barrier = pltpu.get_barrier_semaphore()

    def greet(**dev):
        pl.semaphore_signal(
            barrier, inc=1, device_id=dev, device_id_type=pl.DeviceIdType.MESH
        )

    def along_z(i):
        other = (z + i) % Z
        return {"dp": other % 8, "tm": (other // 8) * 8 + q}

    for i in range(1, Z):
        greet(**along_z(i))
    for i in range(1, 8):
        greet(tm=z_hi * 8 + (q + i) % 8)
    for i in range(4):
        if i:
            greet(mp=(mp + i) % 4)
            greet(tm=(1 - z_hi) * 8 + q, mp=(mp + i) % 4)
        greet(tm=tm_up, mp=(mp + i) % 4)
        greet(tm=tm_down, mp=(mp + i) % 4)

    packf[...] = jnp.zeros_like(packf)
    packf[0, 0:7, :] = subw[...].astype(F32)
    packf[0, 7:19, :] = outw[...].astype(F32)
    packf[1, 0:12, :] = valw[...].astype(F32)
    packf[1, 12:24, :] = gatw[...].astype(F32)
    pack[...] = packf[...].astype(BF16)

    position = (
        seg * 40960
        + lax.broadcasted_iota(jnp.int32, (328, 128), 0) * 128
        + lax.broadcasted_iota(jnp.int32, (328, 128), 1)
    )

    def log_mel(start, count, steps):
        wide = jnp.concatenate(
            [wbuf[pl.ds(5 * start + c, count, stride=5), :] for c in range(7)], axis=1
        )
        frames = jnp.concatenate(
            [
                (pltpu.roll(wide, 896 - HOP * j, 1) if j else wide)[:, :512]
                for j in steps
            ],
            axis=0,
        )
        spectrum = exact_dot(frames, table[...])
        power = (
            spectrum[:, :256] * spectrum[:, :256] + spectrum[:, 256:] * spectrum[:, 256:]
        )
        energy = jnp.log(exact_dot(power, filters[...]) + 1e-06)
        for k, j in enumerate(steps):
            lg[j, start : start + count, :] = energy[k * count : k * count + count]

    loads[0].wait()
    wbuf[0:320] = jnp.where(position[:320] < length, wav[...], 0.0)
    wbuf[320:328] = jnp.zeros((8, 128), F32)
    loads[1].wait()
    loads[2].wait()
    log_mel(0, 64, range(STRIDE))

    pl.semaphore_wait(barrier, 15 + 7 + 3 + 3 + 8)

    swap = remote(pack.at[1 - core], got, c_s, c_r, tm=twin)
    swap.start()
    prev_mp = (mp + 3) % 4
    prev_tm = (tm + 15 + (mp + 3) // 4) % 16
    halo_copy = remote(wav.at[0:8], halo, h_s, h_r, tm=prev_tm, mp=prev_mp)
    halo_copy.start()

    swap.wait_recv()
    mine, other = packf[core], got[...].astype(F32)
    first = jnp.where(core == 0, mine, other)
    second = jnp.where(core == 0, other, mine)

    @pl.when(core == 0)
    def _():
        own48[0:7] = first[0:7]
        own48[7:14] = second[0:7]
        own48[14:16] = jnp.zeros((2, 384), F32)
        own48[16:28] = first[7:19]
        own48[28:40] = second[7:19]
        own48[40:48] = jnp.zeros((8, 384), F32)

    @pl.when(core == 1)
    def _():
        own48[0:12] = first[0:12]
        own48[12:24] = second[0:12]
        own48[24:36] = first[12:24]
        own48[36:48] = second[12:24]

    def on(which):
        return pl.when(core == which)

    for c in range(2):
        @on(c)
        def _(c=c):
            for j in range(3):
                w[3 * c + j, z % 4, z // 4, x] = own48[16 * j : 16 * j + 16].astype(BF16)

    def push(ref, ssem, rsem, **dev):
        remote(ref, ref, ssem, rsem, **dev).start()

    FAR = (8, 4, 12)
    CLOSE = (4, 12, 3, 13, 2, 14, 1, 15)
    APART = (8, 7, 9, 6, 10, 5, 11)
    NEAR = {1: pl.ds(0, 4), 15: pl.ds(0, 4), 2: pl.ds(0, 2), 14: pl.ds(2, 2)}

    def own_tile(b):
        return w.at[b, z % 4, z // 4] if b == 5 else w.at[b, z % 4, z // 4, x]

    def own_class(b, part):
        return w.at[b, z % 4, part] if b == 5 else w.at[b, z % 4, part, x]

    def tiles(b, n):
        if n in (7, 8, 15):
            return vw.at[pl.ds(0, n), pl.ds(0, 16)]
        if n == 3:
            return w.at[b, 0, 0, pl.ds(0, 3)]
        if n == 12:
            return w.at[b, 0, pl.ds(0, 3)]
        return w.at[b, pl.ds(0, n // 16)]

    def along_x(i):
        return {"tm": z_hi * 8 + ((x + i) % 4) * 2 + core}

    def send_far(b):
        for i in FAR:
            push(own_tile(b), z_s.at[b], far_r.at[b], **along_z(i))

    def send_all():
        for i in CLOSE:
            push(own_tile(0), z_s.at[0], near_r.at[0], **along_z(i))
        for i in APART:
            push(own_tile(0), z_s.at[0], far_r.at[0], **along_z(i))

    def pass_on(offsets):
        for i in offsets:
            at = (z + Z - i) % Z
            ref = w.at[0, at % 4, at // 4, x]
            for k in (2, 1, 3):
                push(ref, x_s.at[0], x_r.at[0], **along_x(k))

    def all_over_x():
        arrived(tiles(0, 8), near_r.at[0])
        pass_on((0,) + CLOSE)
        arrived(tiles(0, 7), far_r.at[0])
        pass_on(APART)
        push(column(0, 0), sib_s.at[0], sib_r.at[0], tm=twin)

    def send_near(b):
        arrived(tiles(b, 12 if b == 5 else 3), far_r.at[b])
        for i, part in NEAR.items():
            push(own_class(b, part), z_s.at[6 if b == 5 else b], near_r.at[b], **along_z(i))

    def column(b, i):
        return w.at[b, :, :, (x + 4 - i) % 4]

    def send_x(b):
        arrived(tiles(b, 12), near_r.at[b])
        for i in (2, 1, 3):
            push(column(b, 0), x_s.at[b], x_r.at[b], **along_x(i))
        push(column(b, 0), sib_s.at[b], sib_r.at[b], tm=twin)

    def send_twin(b):
        arrived(tiles(b, 48), x_r.at[b])
        for i in (1, 3, 2):
            push(column(b, i), sib_s.at[b], sib_r.at[b], tm=twin)

    def first_x():
        ref = w.at[5, z % 4, z // 4, x]
        for i in (2, 1, 3):
            push(ref, x_s.at[5], x_r.at[5], **along_x(i))

    def far_5():
        arrived(tiles(5, 3), x_r.at[5])
        send_far(5)

    def twin_5():
        arrived(tiles(5, 48), near_r.at[5])
        push(w.at[5], sib_s.at[5], sib_r.at[5], tm=twin)

    def from_twin(b):
        arrived(w.at[b], sib_r.at[b])

    halo_copy.wait_recv()
    wbuf[320:328] = jnp.where(position[320:328] < length, halo[...], 0.0)
    log_mel(56, 8, (2, 3))
    row = lax.broadcasted_iota(jnp.int32, (256, MEL), 0)
    valid_mel = seg * 256 + (row % 64) * 4 + row // 64 < length // HOP
    log_energy = jnp.concatenate([lg[j] for j in range(STRIDE)], axis=0)
    kept = jnp.where(valid_mel, log_energy, 0.0)
    place = z_hi * 4 + mp
    ma[place] = jnp.concatenate(
        [
            jnp.sum(kept, axis=0, keepdims=True),
            jnp.sum(kept * kept, axis=0, keepdims=True),
            jnp.zeros((6, MEL), F32),
        ],
        axis=0,
    )

    for i in (4, 5, 6, 7, 3, 2, 1):
        away = (place + i) % 8
        push(ma.at[place], ma_s, ma_r, tm=(away // 4) * 8 + q, mp=away % 4)

    @on(0)
    def _():
        send_all()

    @on(1)
    def _():
        first_x()
        send_far(3)
        send_far(4)

    own = pl.ds(pl.multiple_of(8 + mp * 64, 8), 64)
    for j in range(STRIDE):
        le[j, own, :] = log_energy[j * 64 : j * 64 + 64]

    ours = le.at[:, own, :]
    next_halo = le.at[:, pl.ds(256, 8), :], le.at[:, pl.ds(0, 8), :]

    @pl.when(mp == 3)
    def _():
        for i in range(4):
            remote(*next_halo, lh_s, lh_r, tm=tm_up, mp=(mp + i) % 4).start()

    for i in (2, 1, 3):
        push(ours, le_s, le_r, mp=(mp + i) % 4)
    arrived(ma.at[pl.ds(0, 7)], ma_r)
    total = ma[0]
    for i in range(1, 8):
        total = total + ma[i]
    mb[q] = total
    for i in range(1, 8):
        push(mb.at[q], mb_s, mb_r, tm=z_hi * 8 + (q + i) % 8)

    @on(0)
    def _():
        all_over_x()

    @on(1)
    def _():
        far_5()
        send_near(3)
        send_near(4)

    arrived(mb.at[pl.ds(0, 7)], mb_r)
    total = mb[0]
    for i in range(1, 8):
        total = total + mb[i]
    count = (length // HOP).astype(F32)
    mel_mean = total[0:1] / count
    mel_var = total[1:2] / count - mel_mean * mel_mean
    mel_scale = lax.rsqrt(mel_var + 1e-05)
    arrived(le.at[:, pl.ds(0, 192), :], le_r)
    arrived(le.at[:, pl.ds(0, 8), :], lh_r)
    time = tm * 256 - 8 + lax.broadcasted_iota(jnp.int32, (264, MEL), 0)
    for j in range(STRIDE):
        known = (time >= 0) & (time * 4 + j < length // HOP)
        nmf[j] = jnp.where(known, (le[j] - mel_mean) * mel_scale, 0.0)

    @on(0)
    def _():
        send_far(1)
        send_far(2)
        send_twin(0)

    @on(1)
    def _():
        send_near(5)
        send_x(3)
        send_x(4)
        from_twin(0)

    for s in range(Z):
        for i in range(4):
            at = (s % 2) * 8 + s // 2
            sf[56 * s + 14 * i : 56 * s + 14 * i + 14, :] = w[0, at % 4, at // 4, i].astype(
                F32
            )[0:14]
    stacked = jnp.concatenate(
        [nmf[j, 7:263] for j in range(1, STRIDE)] + [nmf[j, 8:264] for j in range(STRIDE)],
        axis=1,
    ).astype(BF16)
    feats[mp] = jnp.dot(
        stacked, sf[...].astype(BF16), preferred_element_type=F32
    ).astype(BF16)

    for i in (2, 1, 3):
        push(feats.at[mp], ag_s, ag_r, mp=(mp + i) % 4)

    @on(0)
    def _():
        send_near(1)
        send_near(2)
        send_x(1)
        send_x(2)

    @on(1)
    def _():
        twin_5()
        send_twin(3)
        send_twin(4)

    arrived(feats.at[pl.ds(0, 3)], ag_r)

    @pl.loop(0, 8, unroll=2)
    def _(b):
        rows = pl.ds(pl.multiple_of(b * 32, 32), 32)
        wide = jnp.concatenate([feats[g, rows, :] for g in range(4)], axis=1).astype(F32)
        centered = wide - jnp.mean(wide, axis=1, keepdims=True)
        spread = jnp.mean(centered * centered, axis=1, keepdims=True)
        normed[rows, :] = (centered * lax.rsqrt(spread + 1e-05)).astype(BF16)

    @on(0)
    def _():
        for b in (5, 3, 4):
            from_twin(b)

    @pl.loop(0, Z)
    def _(s):
        value, gate = [], []
        at = (s % 2) * 8 + s // 2
        for i in range(4):
            top, middle, bottom = (
                w[b, at % 4, at // 4, i].astype(F32) for b in (3, 4, 5)
            )
            value += [top, middle[0:8]]
            gate += [middle[8:16], bottom]
        vw[s] = jnp.concatenate(value, axis=0).astype(BF16)
        gw[s] = jnp.concatenate(gate, axis=0).astype(BF16)

    value_sum = jnp.dot(
        normed[...], vw[...].reshape(1536, 384), preferred_element_type=F32
    )
    gate_sum = jnp.dot(
        normed[...], gw[...].reshape(1536, 384), preferred_element_type=F32
    )
    valid = (
        tm * 256 + lax.broadcasted_iota(jnp.int32, (256, 384), 0)
        < length // (STRIDE * HOP)
    )
    gated = jnp.where(valid, value_sum * jax.nn.sigmoid(gate_sum), 0.0)
    gp[16:272, :] = gated.astype(BF16)

    to_next = remote(
        gp.at[pl.ds(256, 16)], gp.at[pl.ds(0, 16)], gh_s.at[0], gh_r.at[0], tm=tm_up
    )
    to_prev = remote(
        gp.at[pl.ds(16, 16)], gp.at[pl.ds(272, 16)], gh_s.at[1], gh_r.at[1], tm=tm_down
    )
    to_next.start()
    to_prev.start()
    gf[16:272, :] = gp[16:272, :].astype(F32)
    loads[3].wait()

    def depthwise(block, column):
        rows = pl.multiple_of(block * 64, 64)
        lanes = pl.ds(pl.multiple_of(column * 128, 128), 128)
        window = gf[pl.ds(rows, 96), lanes]
        taps = dk[:, lanes]
        out = jnp.zeros((64, 128), F32)
        for p in range(8):
            part = jnp.zeros((72, 128), F32)
            for k in range(4):
                tap = 8 * k + p - 1
                if tap >= 0:
                    part = part + taps[tap : tap + 1] * window[8 * k : 8 * k + 72]
            if p:
                part = pltpu.roll(part, 72 - p, 0)
            out = out + part[:64]
        moved = out * scale[lanes].reshape(1, 128) + shift[lanes].reshape(1, 128)
        act[pl.ds(rows, 64), lanes] = (moved * jax.nn.sigmoid(moved)).astype(BF16)

    @pl.loop(0, 6)
    def _(b):
        depthwise(b // 3 + 1, b % 3)

    @on(0)
    def _():
        send_twin(1)
        send_twin(2)

    @on(1)
    def _():
        from_twin(1)
        from_twin(2)

    @pl.loop(0, Z)
    def _(s):
        rows = []
        at = (s % 2) * 8 + s // 2
        for i in range(4):
            rows += [
                w[1, at % 4, at // 4, i].astype(F32),
                w[2, at % 4, at // 4, i].astype(F32)[0:8],
            ]
        ow[s] = jnp.concatenate(rows, axis=0).astype(BF16)

    def partial(rows, g):
        block = ow[pl.ds(g * 4, 4)].reshape(384, 384)
        return lax.dot_general(
            rows, block, NT, preferred_element_type=F32
        ).astype(BF16)

    def scatter(i, start, rows):
        part = pl.ds(start, rows)
        remote(
            ps.at[i, part], rs.at[i, part], rs_s, rs_r, mp=(mp + i) % 4
        ).start()

    inner = act[64:192, :]
    for i in (2, 1, 3):
        ps[i, 64:192] = partial(inner, (mp + i) % 4)
        scatter(i, 64, 128)

    to_next.wait_recv()
    to_prev.wait_recv()
    gf[0:16, :] = jnp.where(tm == 0, 0.0, gp[0:16, :].astype(F32))
    gf[272:288, :] = jnp.where(tm == 15, 0.0, gp[272:288, :].astype(F32))

    @pl.loop(0, 6)
    def _(b):
        depthwise((b // 3) * 3, b % 3)

    outer = jnp.concatenate([act[0:64, :], act[192:256, :]], axis=0)
    for i in (2, 1, 3):
        part = partial(outer, (mp + i) % 4)
        ps[i, 0:64] = part[0:64]
        ps[i, 192:256] = part[64:128]
        scatter(i, 0, 64)
        scatter(i, 192, 64)
    summed = partial(act[...], mp).astype(F32)
    arrived(rs.at[pl.ds(1, 3)], rs_r)
    for i in range(1, 4):
        summed = summed + rs[i].astype(F32)
    out_ref[...] = jnp.where(valid, feats[mp].astype(F32) + summed, 0.0).astype(BF16)

    halo_copy.wait_send()
    swap.wait_send()
    left(ma.at[pl.ds(0, 7)], ma_s)
    left(mb.at[pl.ds(0, 7)], mb_s)
    left(le.at[:, pl.ds(0, 192), :], le_s)
    left(feats.at[pl.ds(0, 3)], ag_s)
    left(rs.at[pl.ds(1, 3)], rs_s)

    @pl.when(mp == 3)
    def _():
        left(le.at[:, pl.ds(0, 32), :], lh_s)

    to_next.wait_send()
    to_prev.wait_send()

    for c in range(2):
        @on(c)
        def _(c=c):
            for b in range(3 * c, 3 * c + 3):
                if b == 5:
                    left(tiles(b, 12), z_s.at[b])
                    left(tiles(b, 48), z_s.at[6])
                    left(tiles(b, 3), x_s.at[b])
                else:
                    left(tiles(b, 15), z_s.at[b])
                    left(tiles(b, 48), x_s.at[b])
                left(w.at[b], sib_s.at[b])


def shards(
    waveform, lengths, sub_weight, value_weight, gate_weight, out_weight,
    depth_kernel, norm_scale, norm_shift,
):
    vmem = pl.BlockSpec(memory_space=pltpu.VMEM)
    hbm = pl.BlockSpec(memory_space=pltpu.HBM)
    dma = pltpu.SemaphoreType.DMA
    encoded = pl.pallas_call(
        kernel,
        out_shape=pltpu.VMEM((256, 384), BF16),
        in_specs=[pl.BlockSpec(memory_space=pltpu.SMEM)] + [vmem] * 4 + [hbm] * 2 + [vmem] * 2 + [hbm] * 2,
        out_specs=vmem,
        scratch_shapes=[
            pltpu.VMEM((320, 128), F32),
            pltpu.VMEM((KERNEL, 384), F32),
            pltpu.VMEM((512, 512), F32),
            pltpu.VMEM((256, MEL), F32),
            pltpu.VMEM((328, 128), F32),
            pltpu.VMEM((8, 128), F32),
            pltpu.VMEM((4, 64, 128), F32),
            pltpu.VMEM((2, 32, 384), BF16),
            pltpu.VMEM((2, 32, 384), F32),
            pltpu.VMEM((32, 384), BF16),
            pltpu.VMEM((48, 384), F32),
            pltpu.VMEM((6, 4, 4, 4, 16, 384), BF16),
            pltpu.VMEM((896, 384), F32),
            pltpu.VMEM((Z, 96, 384), BF16),
            pltpu.VMEM((Z, 96, 384), BF16),
            pltpu.VMEM((Z, 96, 384), BF16),
            pltpu.VMEM((8, 8, 128), F32),
            pltpu.VMEM((8, 8, 128), F32),
            pltpu.VMEM((4, 264, 128), F32),
            pltpu.VMEM((4, 264, 128), F32),
            pltpu.VMEM((4, 256, 384), BF16),
            pltpu.VMEM((256, 1536), BF16),
            pltpu.VMEM((288, 384), BF16),
            pltpu.VMEM((288, 384), F32),
            pltpu.VMEM((256, 384), BF16),
            pltpu.VMEM((4, 256, 384), BF16),
            pltpu.VMEM((4, 256, 384), BF16),
            dma((4,)),
            dma, dma,
            dma, dma,
            dma, dma,
            dma, dma,
            dma, dma,
            dma, dma,
            dma, dma,
            dma((2,)), dma((2,)),
            dma, dma,
            dma((7,)), dma((6,)), dma((6,)),
            dma((6,)), dma((6,)),
            dma((6,)), dma((6,)),
        ],
        compiler_params=pltpu.CompilerParams(
            collective_id=0, has_side_effects=True, vmem_limit_bytes=60 * 1024 * 1024
        ),
    )(
        lengths,
        sub_weight,
        value_weight,
        gate_weight,
        out_weight.T,
        waveform.reshape(320, 128),
        depth_kernel,
        norm_scale,
        norm_shift,
        jnp.asarray(fourier_table()),
        jnp.asarray(mel_filters()),
    )
    return encoded[None]


def solution(mesh):
    placed = (
        P("dp", ("tm", "mp")),
        P("dp"),
        P(("dp", "tm"), "mp"),
        P(("dp", "tm"), "mp"),
        P(("dp", "tm"), "mp"),
        P("mp", ("dp", "tm")),
        P(None, "mp"),
        P("mp"),
        P("mp"),
    )
    return jax.shard_map(
        shards, mesh=mesh, in_specs=placed, out_specs=P("dp", "tm", "mp"), check_vma=False
    )
```

```python
import math

import jax
import jax.numpy as jnp
import numpy as np
from jax import lax
from jax.experimental import pallas as pl
from jax.experimental.pallas import tpu as pltpu
from jax.sharding import PartitionSpec as P

MEL = 128
WIN = 400
HOP = 160
STRIDE = 4
KERNEL = 31
BINS = 201
F32 = jnp.float32
BF16 = jnp.bfloat16
Z = 16
NT = (((1,), (1,)), ((), ()))


def mel_filters():
    mel_top = 2595.0 * math.log10(1.0 + 8000.0 / 700.0)
    borders = np.asarray(
        [
            700.0 * (10.0 ** (i * mel_top / (MEL + 1) / 2595.0) - 1.0) * WIN / 16000.0
            for i in range(MEL + 2)
        ],
        np.float32,
    )
    centers = np.arange(BINS, dtype=np.float32)[:, None]
    middle = borders[1:-1][None, :]
    lower = np.minimum(borders[:-2], borders[1:-1] - np.float32(1.0))[None, :]
    upper = np.maximum(borders[2:], borders[1:-1] + np.float32(1.0))[None, :]
    rising = (centers - lower) / (middle - lower)
    falling = (upper - centers) / (upper - middle)
    full = np.zeros((256, MEL), np.float32)
    full[:BINS] = np.maximum(np.float32(0.0), np.minimum(rising, falling))
    return full


def fourier_table():
    n = np.arange(WIN)
    window = 0.5 - 0.5 * np.cos(2.0 * np.pi * n / WIN)
    phases = 2.0 * np.pi * ((n[:, None] * np.arange(BINS)[None, :]) % WIN) / WIN
    full = np.zeros((512, 512), np.float32)
    full[:WIN, :BINS] = window[:, None] * np.cos(phases)
    full[:WIN, 256 : 256 + BINS] = window[:, None] * np.sin(phases)
    return full


def exact_dot(a, b):
    return jnp.dot(a, b, precision=lax.Precision.HIGHEST, preferred_element_type=F32)


def kernel(
    len_ref, subw, valw, gatw, outw, wav_hbm, dk_hbm, scale, shift, table_hbm, filters_hbm,
    out_ref,
    wav, dk, table, filters, wbuf, halo, lg, pack, packf, got, own48, w, sf, vw, gw, ow,
    ma, mb, le, nmf, feats, normed, gp, gf, act, ps, rs,
    in_s, h_s, h_r, c_s, c_r, ma_s, ma_r, mb_s, mb_r, le_s, le_r, lh_s, lh_r, ag_s, ag_r,
    gh_s, gh_r, rs_s, rs_r, z_s, far_r, near_r, x_s, x_r, sib_s, sib_r,
):
    dp = lax.axis_index("dp")
    tm = lax.axis_index("tm")
    mp = lax.axis_index("mp")
    z_hi = tm // 8
    q = tm % 8
    x = q // 2
    core = tm % 2
    z = z_hi * 8 + dp
    length = len_ref[0]
    seg = tm * 4 + mp
    tm_up, tm_down = (tm + 1) % 16, (tm + 15) % 16
    twin = tm + 1 - 2 * core

    def remote(src, dst, ssem, rsem, **dev):
        return pltpu.make_async_remote_copy(
            src_ref=src, dst_ref=dst, send_sem=ssem, recv_sem=rsem,
            device_id=dev, device_id_type=pl.DeviceIdType.MESH,
        )

    def arrived(ref, rsem):
        remote(ref, ref, c_s, rsem, tm=twin).wait_recv()

    def left(ref, ssem):
        remote(ref, ref, ssem, c_r, tm=twin).wait_send()

    loads = [
        pltpu.make_async_copy(there, here, in_s.at[i])
        for i, (there, here) in enumerate(
            [(wav_hbm, wav), (table_hbm, table), (filters_hbm, filters), (dk_hbm, dk)]
        )
    ]
    for load in loads:
        load.start()

    barrier = pltpu.get_barrier_semaphore()

    def greet(**dev):
        pl.semaphore_signal(
            barrier, inc=1, device_id=dev, device_id_type=pl.DeviceIdType.MESH
        )

    def along_z(i):
        other = (z + i) % Z
        return {"dp": other % 8, "tm": (other // 8) * 8 + q}

    for i in range(1, Z):
        greet(**along_z(i))
    for i in range(1, 8):
        greet(tm=z_hi * 8 + (q + i) % 8)
    for i in range(4):
        if i:
            greet(mp=(mp + i) % 4)
            greet(tm=(1 - z_hi) * 8 + q, mp=(mp + i) % 4)
        greet(tm=tm_up, mp=(mp + i) % 4)
        greet(tm=tm_down, mp=(mp + i) % 4)

    packf[...] = jnp.zeros_like(packf)
    packf[0, 0:7, :] = subw[...].astype(F32)
    packf[0, 7:19, :] = outw[...].astype(F32)
    packf[1, 0:12, :] = valw[...].astype(F32)
    packf[1, 12:24, :] = gatw[...].astype(F32)
    pack[...] = packf[...].astype(BF16)

    position = (
        seg * 40960
        + lax.broadcasted_iota(jnp.int32, (328, 128), 0) * 128
        + lax.broadcasted_iota(jnp.int32, (328, 128), 1)
    )

    def log_mel(start, count, steps):
        wide = jnp.concatenate(
            [wbuf[pl.ds(5 * start + c, count, stride=5), :] for c in range(7)], axis=1
        )
        frames = jnp.concatenate(
            [
                (pltpu.roll(wide, 896 - HOP * j, 1) if j else wide)[:, :512]
                for j in steps
            ],
            axis=0,
        )
        spectrum = exact_dot(frames, table[...])
        power = (
            spectrum[:, :256] * spectrum[:, :256] + spectrum[:, 256:] * spectrum[:, 256:]
        )
        energy = jnp.log(exact_dot(power, filters[...]) + 1e-06)
        for k, j in enumerate(steps):
            lg[j, start : start + count, :] = energy[k * count : k * count + count]

    loads[0].wait()
    wbuf[0:320] = jnp.where(position[:320] < length, wav[...], 0.0)
    wbuf[320:328] = jnp.zeros((8, 128), F32)
    loads[1].wait()
    loads[2].wait()
    log_mel(0, 64, range(STRIDE))

    pl.semaphore_wait(barrier, 15 + 7 + 3 + 3 + 8)

    swap = remote(pack.at[1 - core], got, c_s, c_r, tm=twin)
    swap.start()
    prev_mp = (mp + 3) % 4
    prev_tm = (tm + 15 + (mp + 3) // 4) % 16
    halo_copy = remote(wav.at[0:8], halo, h_s, h_r, tm=prev_tm, mp=prev_mp)
    halo_copy.start()

    swap.wait_recv()
    mine, other = packf[core], got[...].astype(F32)
    first = jnp.where(core == 0, mine, other)
    second = jnp.where(core == 0, other, mine)

    @pl.when(core == 0)
    def _():
        own48[0:7] = first[0:7]
        own48[7:14] = second[0:7]
        own48[14:16] = jnp.zeros((2, 384), F32)
        own48[16:28] = first[7:19]
        own48[28:40] = second[7:19]
        own48[40:48] = jnp.zeros((8, 384), F32)

    @pl.when(core == 1)
    def _():
        own48[0:12] = first[0:12]
        own48[12:24] = second[0:12]
        own48[24:36] = first[12:24]
        own48[36:48] = second[12:24]

    def on(which):
        return pl.when(core == which)

    for c in range(2):
        @on(c)
        def _(c=c):
            for j in range(3):
                w[3 * c + j, z % 4, z // 4, x] = own48[16 * j : 16 * j + 16].astype(BF16)

    def push(ref, ssem, rsem, **dev):
        remote(ref, ref, ssem, rsem, **dev).start()

    FAR = (8, 4, 12)
    CLOSE = (4, 12, 3, 13, 2, 14, 1, 15)
    APART = (8, 7, 9, 6, 10, 5, 11)
    NEAR = {1: pl.ds(0, 4), 15: pl.ds(0, 4), 2: pl.ds(0, 2), 14: pl.ds(2, 2)}

    def own_tile(b):
        return w.at[b, z % 4, z // 4] if b == 5 else w.at[b, z % 4, z // 4, x]

    def own_class(b, part):
        return w.at[b, z % 4, part] if b == 5 else w.at[b, z % 4, part, x]

    def tiles(b, n):
        if n in (7, 8, 15):
            return vw.at[pl.ds(0, n), pl.ds(0, 16)]
        if n == 3:
            return w.at[b, 0, 0, pl.ds(0, 3)]
        if n == 12:
            return w.at[b, 0, pl.ds(0, 3)]
        return w.at[b, pl.ds(0, n // 16)]

    def along_x(i):
        return {"tm": z_hi * 8 + ((x + i) % 4) * 2 + core}

    def send_far(b):
        for i in FAR:
            push(own_tile(b), z_s.at[b], far_r.at[b], **along_z(i))

    def send_close():
        for i in CLOSE:
            push(own_tile(0), z_s.at[0], near_r.at[0], **along_z(i))

    def send_apart():
        for i in APART:
            push(own_tile(0), z_s.at[0], far_r.at[0], **along_z(i))

    def pass_on(offsets):
        for i in offsets:
            at = (z + Z - i) % Z
            ref = w.at[0, at % 4, at // 4, x]
            for k in (2, 1, 3):
                push(ref, x_s.at[0], x_r.at[0], **along_x(k))

    def all_over_x():
        arrived(tiles(0, 8), near_r.at[0])
        pass_on((0,) + CLOSE)
        arrived(tiles(0, 7), far_r.at[0])
        pass_on(APART)
        push(column(0, 0), sib_s.at[0], sib_r.at[0], tm=twin)

    def send_near(b):
        arrived(tiles(b, 12 if b == 5 else 3), far_r.at[b])
        for i, part in NEAR.items():
            push(own_class(b, part), z_s.at[6 if b == 5 else b], near_r.at[b], **along_z(i))

    def column(b, i):
        return w.at[b, :, :, (x + 4 - i) % 4]

    def send_x(b):
        arrived(tiles(b, 12), near_r.at[b])
        for i in (2, 1, 3):
            push(column(b, 0), x_s.at[b], x_r.at[b], **along_x(i))
        push(column(b, 0), sib_s.at[b], sib_r.at[b], tm=twin)

    def send_twin(b):
        arrived(tiles(b, 48), x_r.at[b])
        for i in (1, 3, 2):
            push(column(b, i), sib_s.at[b], sib_r.at[b], tm=twin)

    def first_x():
        ref = w.at[5, z % 4, z // 4, x]
        for i in (2, 1, 3):
            push(ref, x_s.at[5], x_r.at[5], **along_x(i))

    def far_5():
        arrived(tiles(5, 3), x_r.at[5])
        send_far(5)

    def twin_5():
        arrived(tiles(5, 48), near_r.at[5])
        push(w.at[5], sib_s.at[5], sib_r.at[5], tm=twin)

    def from_twin(b):
        arrived(w.at[b], sib_r.at[b])

    @on(0)
    def _():
        send_close()

    halo_copy.wait_recv()
    wbuf[320:328] = jnp.where(position[320:328] < length, halo[...], 0.0)
    log_mel(56, 8, (2, 3))
    row = lax.broadcasted_iota(jnp.int32, (256, MEL), 0)
    valid_mel = seg * 256 + (row % 64) * 4 + row // 64 < length // HOP
    log_energy = jnp.concatenate([lg[j] for j in range(STRIDE)], axis=0)
    kept = jnp.where(valid_mel, log_energy, 0.0)
    place = z_hi * 4 + mp
    ma[place] = jnp.concatenate(
        [
            jnp.sum(kept, axis=0, keepdims=True),
            jnp.sum(kept * kept, axis=0, keepdims=True),
            jnp.zeros((6, MEL), F32),
        ],
        axis=0,
    )

    for i in (4, 5, 6, 7, 3, 2, 1):
        away = (place + i) % 8
        push(ma.at[place], ma_s, ma_r, tm=(away // 4) * 8 + q, mp=away % 4)

    @on(0)
    def _():
        send_apart()
        send_far(1)
        send_far(2)

    @on(1)
    def _():
        first_x()
        send_far(3)
        send_far(4)

    own = pl.ds(pl.multiple_of(8 + mp * 64, 8), 64)
    for j in range(STRIDE):
        le[j, own, :] = log_energy[j * 64 : j * 64 + 64]

    ours = le.at[:, own, :]
    next_halo = le.at[:, pl.ds(256, 8), :], le.at[:, pl.ds(0, 8), :]

    @pl.when(mp == 3)
    def _():
        for i in range(4):
            remote(*next_halo, lh_s, lh_r, tm=tm_up, mp=(mp + i) % 4).start()

    for i in (2, 1, 3):
        push(ours, le_s, le_r, mp=(mp + i) % 4)
    arrived(ma.at[pl.ds(0, 7)], ma_r)
    total = ma[0]
    for i in range(1, 8):
        total = total + ma[i]
    mb[q] = total
    for i in range(1, 8):
        push(mb.at[q], mb_s, mb_r, tm=z_hi * 8 + (q + i) % 8)

    @on(0)
    def _():
        all_over_x()
        send_near(1)
        send_near(2)

    @on(1)
    def _():
        far_5()
        send_near(3)
        send_near(4)

    arrived(mb.at[pl.ds(0, 7)], mb_r)
    total = mb[0]
    for i in range(1, 8):
        total = total + mb[i]
    count = (length // HOP).astype(F32)
    mel_mean = total[0:1] / count
    mel_var = total[1:2] / count - mel_mean * mel_mean
    mel_scale = lax.rsqrt(mel_var + 1e-05)
    arrived(le.at[:, pl.ds(0, 192), :], le_r)
    arrived(le.at[:, pl.ds(0, 8), :], lh_r)
    time = tm * 256 - 8 + lax.broadcasted_iota(jnp.int32, (264, MEL), 0)
    for j in range(STRIDE):
        known = (time >= 0) & (time * 4 + j < length // HOP)
        nmf[j] = jnp.where(known, (le[j] - mel_mean) * mel_scale, 0.0)

    @on(0)
    def _():
        send_twin(0)

    @on(1)
    def _():
        send_near(5)
        send_x(3)
        send_x(4)
        from_twin(0)

    for s in range(Z):
        for i in range(4):
            at = (s % 2) * 8 + s // 2
            sf[56 * s + 14 * i : 56 * s + 14 * i + 14, :] = w[0, at % 4, at // 4, i].astype(
                F32
            )[0:14]
    stacked = jnp.concatenate(
        [nmf[j, 7:263] for j in range(1, STRIDE)] + [nmf[j, 8:264] for j in range(STRIDE)],
        axis=1,
    ).astype(BF16)
    feats[mp] = jnp.dot(
        stacked, sf[...].astype(BF16), preferred_element_type=F32
    ).astype(BF16)

    for i in (2, 1, 3):
        push(feats.at[mp], ag_s, ag_r, mp=(mp + i) % 4)

    @on(0)
    def _():
        send_x(1)
        from_twin(5)
        from_twin(3)
        send_x(2)

    @on(1)
    def _():
        twin_5()
        send_twin(3)
        send_twin(4)

    arrived(feats.at[pl.ds(0, 3)], ag_r)

    @pl.loop(0, 8, unroll=2)
    def _(b):
        rows = pl.ds(pl.multiple_of(b * 32, 32), 32)
        wide = jnp.concatenate([feats[g, rows, :] for g in range(4)], axis=1).astype(F32)
        centered = wide - jnp.mean(wide, axis=1, keepdims=True)
        spread = jnp.mean(centered * centered, axis=1, keepdims=True)
        normed[rows, :] = (centered * lax.rsqrt(spread + 1e-05)).astype(BF16)

    @on(0)
    def _():
        from_twin(4)

    @pl.loop(0, Z)
    def _(s):
        value, gate = [], []
        at = (s % 2) * 8 + s // 2
        for i in range(4):
            top, middle, bottom = (
                w[b, at % 4, at // 4, i].astype(F32) for b in (3, 4, 5)
            )
            value += [top, middle[0:8]]
            gate += [middle[8:16], bottom]
        vw[s] = jnp.concatenate(value, axis=0).astype(BF16)
        gw[s] = jnp.concatenate(gate, axis=0).astype(BF16)

    value_sum = jnp.dot(
        normed[...], vw[...].reshape(1536, 384), preferred_element_type=F32
    )
    gate_sum = jnp.dot(
        normed[...], gw[...].reshape(1536, 384), preferred_element_type=F32
    )
    valid = (
        tm * 256 + lax.broadcasted_iota(jnp.int32, (256, 384), 0)
        < length // (STRIDE * HOP)
    )
    gated = jnp.where(valid, value_sum * jax.nn.sigmoid(gate_sum), 0.0)
    gp[16:272, :] = gated.astype(BF16)

    to_next = remote(
        gp.at[pl.ds(256, 16)], gp.at[pl.ds(0, 16)], gh_s.at[0], gh_r.at[0], tm=tm_up
    )
    to_prev = remote(
        gp.at[pl.ds(16, 16)], gp.at[pl.ds(272, 16)], gh_s.at[1], gh_r.at[1], tm=tm_down
    )
    to_next.start()
    to_prev.start()
    gf[16:272, :] = gp[16:272, :].astype(F32)
    loads[3].wait()

    def depthwise(block, column):
        rows = pl.multiple_of(block * 64, 64)
        lanes = pl.ds(pl.multiple_of(column * 128, 128), 128)
        window = gf[pl.ds(rows, 96), lanes]
        taps = dk[:, lanes]
        out = jnp.zeros((64, 128), F32)
        for p in range(8):
            part = jnp.zeros((72, 128), F32)
            for k in range(4):
                tap = 8 * k + p - 1
                if tap >= 0:
                    part = part + taps[tap : tap + 1] * window[8 * k : 8 * k + 72]
            if p:
                part = pltpu.roll(part, 72 - p, 0)
            out = out + part[:64]
        moved = out * scale[lanes].reshape(1, 128) + shift[lanes].reshape(1, 128)
        act[pl.ds(rows, 64), lanes] = (moved * jax.nn.sigmoid(moved)).astype(BF16)

    @pl.loop(0, 6)
    def _(b):
        depthwise(b // 3 + 1, b % 3)

    @on(0)
    def _():
        send_twin(1)
        send_twin(2)

    @on(1)
    def _():
        from_twin(1)
        from_twin(2)

    @pl.loop(0, Z)
    def _(s):
        rows = []
        at = (s % 2) * 8 + s // 2
        for i in range(4):
            rows += [
                w[1, at % 4, at // 4, i].astype(F32),
                w[2, at % 4, at // 4, i].astype(F32)[0:8],
            ]
        ow[s] = jnp.concatenate(rows, axis=0).astype(BF16)

    def partial(rows, g):
        block = ow[pl.ds(g * 4, 4)].reshape(384, 384)
        return lax.dot_general(
            rows, block, NT, preferred_element_type=F32
        ).astype(BF16)

    def scatter(i, start, rows):
        part = pl.ds(start, rows)
        remote(
            ps.at[i, part], rs.at[i, part], rs_s, rs_r, mp=(mp + i) % 4
        ).start()

    inner = act[64:192, :]
    for i in (2, 1, 3):
        ps[i, 64:192] = partial(inner, (mp + i) % 4)
        scatter(i, 64, 128)

    to_next.wait_recv()
    to_prev.wait_recv()
    gf[0:16, :] = jnp.where(tm == 0, 0.0, gp[0:16, :].astype(F32))
    gf[272:288, :] = jnp.where(tm == 15, 0.0, gp[272:288, :].astype(F32))

    @pl.loop(0, 6)
    def _(b):
        depthwise((b // 3) * 3, b % 3)

    outer = jnp.concatenate([act[0:64, :], act[192:256, :]], axis=0)
    for i in (2, 1, 3):
        part = partial(outer, (mp + i) % 4)
        ps[i, 0:64] = part[0:64]
        ps[i, 192:256] = part[64:128]
        scatter(i, 0, 64)
        scatter(i, 192, 64)
    summed = partial(act[...], mp).astype(F32)
    arrived(rs.at[pl.ds(1, 3)], rs_r)
    for i in range(1, 4):
        summed = summed + rs[i].astype(F32)
    out_ref[...] = jnp.where(valid, feats[mp].astype(F32) + summed, 0.0).astype(BF16)

    halo_copy.wait_send()
    swap.wait_send()
    left(ma.at[pl.ds(0, 7)], ma_s)
    left(mb.at[pl.ds(0, 7)], mb_s)
    left(le.at[:, pl.ds(0, 192), :], le_s)
    left(feats.at[pl.ds(0, 3)], ag_s)
    left(rs.at[pl.ds(1, 3)], rs_s)

    @pl.when(mp == 3)
    def _():
        left(le.at[:, pl.ds(0, 32), :], lh_s)

    to_next.wait_send()
    to_prev.wait_send()

    for c in range(2):
        @on(c)
        def _(c=c):
            for b in range(3 * c, 3 * c + 3):
                if b == 5:
                    left(tiles(b, 12), z_s.at[b])
                    left(tiles(b, 48), z_s.at[6])
                    left(tiles(b, 3), x_s.at[b])
                else:
                    left(tiles(b, 15), z_s.at[b])
                    left(tiles(b, 48), x_s.at[b])
                left(w.at[b], sib_s.at[b])


def shards(
    waveform, lengths, sub_weight, value_weight, gate_weight, out_weight,
    depth_kernel, norm_scale, norm_shift,
):
    vmem = pl.BlockSpec(memory_space=pltpu.VMEM)
    hbm = pl.BlockSpec(memory_space=pltpu.HBM)
    dma = pltpu.SemaphoreType.DMA
    encoded = pl.pallas_call(
        kernel,
        out_shape=pltpu.VMEM((256, 384), BF16),
        in_specs=[pl.BlockSpec(memory_space=pltpu.SMEM)] + [vmem] * 4 + [hbm] * 2 + [vmem] * 2 + [hbm] * 2,
        out_specs=vmem,
        scratch_shapes=[
            pltpu.VMEM((320, 128), F32),
            pltpu.VMEM((KERNEL, 384), F32),
            pltpu.VMEM((512, 512), F32),
            pltpu.VMEM((256, MEL), F32),
            pltpu.VMEM((328, 128), F32),
            pltpu.VMEM((8, 128), F32),
            pltpu.VMEM((4, 64, 128), F32),
            pltpu.VMEM((2, 32, 384), BF16),
            pltpu.VMEM((2, 32, 384), F32),
            pltpu.VMEM((32, 384), BF16),
            pltpu.VMEM((48, 384), F32),
            pltpu.VMEM((6, 4, 4, 4, 16, 384), BF16),
            pltpu.VMEM((896, 384), F32),
            pltpu.VMEM((Z, 96, 384), BF16),
            pltpu.VMEM((Z, 96, 384), BF16),
            pltpu.VMEM((Z, 96, 384), BF16),
            pltpu.VMEM((8, 8, 128), F32),
            pltpu.VMEM((8, 8, 128), F32),
            pltpu.VMEM((4, 264, 128), F32),
            pltpu.VMEM((4, 264, 128), F32),
            pltpu.VMEM((4, 256, 384), BF16),
            pltpu.VMEM((256, 1536), BF16),
            pltpu.VMEM((288, 384), BF16),
            pltpu.VMEM((288, 384), F32),
            pltpu.VMEM((256, 384), BF16),
            pltpu.VMEM((4, 256, 384), BF16),
            pltpu.VMEM((4, 256, 384), BF16),
            dma((4,)),
            dma, dma,
            dma, dma,
            dma, dma,
            dma, dma,
            dma, dma,
            dma, dma,
            dma, dma,
            dma((2,)), dma((2,)),
            dma, dma,
            dma((7,)), dma((6,)), dma((6,)),
            dma((6,)), dma((6,)),
            dma((6,)), dma((6,)),
        ],
        compiler_params=pltpu.CompilerParams(
            collective_id=0, has_side_effects=True, vmem_limit_bytes=60 * 1024 * 1024
        ),
    )(
        lengths,
        sub_weight,
        value_weight,
        gate_weight,
        out_weight.T,
        waveform.reshape(320, 128),
        depth_kernel,
        norm_scale,
        norm_shift,
        jnp.asarray(fourier_table()),
        jnp.asarray(mel_filters()),
    )
    return encoded[None]


def solution(mesh):
    placed = (
        P("dp", ("tm", "mp")),
        P("dp"),
        P(("dp", "tm"), "mp"),
        P(("dp", "tm"), "mp"),
        P(("dp", "tm"), "mp"),
        P("mp", ("dp", "tm")),
        P(None, "mp"),
        P("mp"),
        P("mp"),
    )
    return jax.shard_map(
        shards, mesh=mesh, in_specs=placed, out_specs=P("dp", "tm", "mp"), check_vma=False
    )
```

```python
import math

import jax
import jax.numpy as jnp
import numpy as np
from jax import lax
from jax.experimental import pallas as pl
from jax.experimental.pallas import tpu as pltpu
from jax.sharding import PartitionSpec as P

MEL = 128
WIN = 400
HOP = 160
STRIDE = 4
KERNEL = 31
BINS = 201
F32 = jnp.float32
BF16 = jnp.bfloat16
Z = 16
NT = (((1,), (1,)), ((), ()))


def mel_filters():
    mel_top = 2595.0 * math.log10(1.0 + 8000.0 / 700.0)
    borders = np.asarray(
        [
            700.0 * (10.0 ** (i * mel_top / (MEL + 1) / 2595.0) - 1.0) * WIN / 16000.0
            for i in range(MEL + 2)
        ],
        np.float32,
    )
    centers = np.arange(BINS, dtype=np.float32)[:, None]
    middle = borders[1:-1][None, :]
    lower = np.minimum(borders[:-2], borders[1:-1] - np.float32(1.0))[None, :]
    upper = np.maximum(borders[2:], borders[1:-1] + np.float32(1.0))[None, :]
    rising = (centers - lower) / (middle - lower)
    falling = (upper - centers) / (upper - middle)
    full = np.zeros((256, MEL), np.float32)
    full[:BINS] = np.maximum(np.float32(0.0), np.minimum(rising, falling))
    return full


def fourier_table():
    n = np.arange(WIN)
    window = 0.5 - 0.5 * np.cos(2.0 * np.pi * n / WIN)
    phases = 2.0 * np.pi * ((n[:, None] * np.arange(BINS)[None, :]) % WIN) / WIN
    full = np.zeros((512, 512), np.float32)
    full[:WIN, :BINS] = window[:, None] * np.cos(phases)
    full[:WIN, 256 : 256 + BINS] = window[:, None] * np.sin(phases)
    return full


def exact_dot(a, b):
    return jnp.dot(a, b, precision=lax.Precision.HIGHEST, preferred_element_type=F32)


def kernel(
    len_ref, subw, valw, gatw, outw, wav_hbm, dk_hbm, scale, shift, table_hbm, filters_hbm,
    out_ref,
    wav, dk, table, filters, wbuf, halo, lg, pack, packf, got, own48, w, sf, vw, gw, ow,
    ma, mb, le, nmf, feats, normed, gp, gf, act, ps, rs,
    in_s, h_s, h_r, c_s, c_r, ma_s, ma_r, mb_s, mb_r, le_s, le_r, lh_s, lh_r, ag_s, ag_r,
    gh_s, gh_r, rs_s, rs_r, z_s, far_r, near_r, x_s, x_r, sib_s, sib_r,
):
    dp = lax.axis_index("dp")
    tm = lax.axis_index("tm")
    mp = lax.axis_index("mp")
    z_hi = tm // 8
    q = tm % 8
    x = q // 2
    core = tm % 2
    z = z_hi * 8 + dp
    length = len_ref[0]
    seg = tm * 4 + mp
    tm_up, tm_down = (tm + 1) % 16, (tm + 15) % 16
    twin = tm + 1 - 2 * core

    def remote(src, dst, ssem, rsem, **dev):
        return pltpu.make_async_remote_copy(
            src_ref=src, dst_ref=dst, send_sem=ssem, recv_sem=rsem,
            device_id=dev, device_id_type=pl.DeviceIdType.MESH,
        )

    def arrived(ref, rsem):
        remote(ref, ref, c_s, rsem, tm=twin).wait_recv()

    def left(ref, ssem):
        remote(ref, ref, ssem, c_r, tm=twin).wait_send()

    loads = [
        pltpu.make_async_copy(there, here, in_s.at[i])
        for i, (there, here) in enumerate(
            [(wav_hbm, wav), (table_hbm, table), (filters_hbm, filters), (dk_hbm, dk)]
        )
    ]
    for load in loads:
        load.start()

    barrier = pltpu.get_barrier_semaphore()

    def greet(**dev):
        pl.semaphore_signal(
            barrier, inc=1, device_id=dev, device_id_type=pl.DeviceIdType.MESH
        )

    def along_z(i):
        other = (z + i) % Z
        return {"dp": other % 8, "tm": (other // 8) * 8 + q}

    for i in range(1, Z):
        greet(**along_z(i))
    for i in range(1, 8):
        greet(tm=z_hi * 8 + (q + i) % 8)
    for i in range(4):
        if i:
            greet(mp=(mp + i) % 4)
            greet(tm=(1 - z_hi) * 8 + q, mp=(mp + i) % 4)
        greet(tm=tm_up, mp=(mp + i) % 4)
        greet(tm=tm_down, mp=(mp + i) % 4)

    packf[...] = jnp.zeros_like(packf)
    packf[0, 0:7, :] = subw[...].astype(F32)
    packf[0, 7:19, :] = outw[...].astype(F32)
    packf[1, 0:12, :] = valw[...].astype(F32)
    packf[1, 12:24, :] = gatw[...].astype(F32)
    pack[...] = packf[...].astype(BF16)

    position = (
        seg * 40960
        + lax.broadcasted_iota(jnp.int32, (328, 128), 0) * 128
        + lax.broadcasted_iota(jnp.int32, (328, 128), 1)
    )

    def log_mel(start, count, steps):
        wide = jnp.concatenate(
            [wbuf[pl.ds(5 * start + c, count, stride=5), :] for c in range(7)], axis=1
        )
        frames = jnp.concatenate(
            [
                (pltpu.roll(wide, 896 - HOP * j, 1) if j else wide)[:, :512]
                for j in steps
            ],
            axis=0,
        )
        spectrum = exact_dot(frames, table[...])
        power = (
            spectrum[:, :256] * spectrum[:, :256] + spectrum[:, 256:] * spectrum[:, 256:]
        )
        energy = jnp.log(exact_dot(power, filters[...]) + 1e-06)
        for k, j in enumerate(steps):
            lg[j, start : start + count, :] = energy[k * count : k * count + count]

    loads[0].wait()
    wbuf[0:320] = jnp.where(position[:320] < length, wav[...], 0.0)
    wbuf[320:328] = jnp.zeros((8, 128), F32)
    loads[1].wait()
    loads[2].wait()
    log_mel(0, 64, range(STRIDE))

    pl.semaphore_wait(barrier, 15 + 7 + 3 + 3 + 8)

    swap = remote(pack.at[1 - core], got, c_s, c_r, tm=twin)
    swap.start()
    prev_mp = (mp + 3) % 4
    prev_tm = (tm + 15 + (mp + 3) // 4) % 16
    halo_copy = remote(wav.at[0:8], halo, h_s, h_r, tm=prev_tm, mp=prev_mp)
    halo_copy.start()

    swap.wait_recv()
    mine, other = packf[core], got[...].astype(F32)
    first = jnp.where(core == 0, mine, other)
    second = jnp.where(core == 0, other, mine)

    @pl.when(core == 0)
    def _():
        own48[0:7] = first[0:7]
        own48[7:14] = second[0:7]
        own48[14:16] = jnp.zeros((2, 384), F32)
        own48[16:28] = first[7:19]
        own48[28:40] = second[7:19]
        own48[40:48] = jnp.zeros((8, 384), F32)

    @pl.when(core == 1)
    def _():
        own48[0:12] = first[0:12]
        own48[12:24] = second[0:12]
        own48[24:36] = first[12:24]
        own48[36:48] = second[12:24]

    def on(which):
        return pl.when(core == which)

    for c in range(2):
        @on(c)
        def _(c=c):
            for j in range(3):
                w[3 * c + j, z % 4, z // 4, x] = own48[16 * j : 16 * j + 16].astype(BF16)

    def push(ref, ssem, rsem, **dev):
        remote(ref, ref, ssem, rsem, **dev).start()

    FAR = (8, 4, 12)
    CLOSE = (4, 12, 3, 13, 2, 14, 1, 15)
    APART = (8, 7, 9, 6, 10, 5, 11)
    NEAR = {1: pl.ds(0, 4), 15: pl.ds(0, 4), 2: pl.ds(0, 2), 14: pl.ds(2, 2)}

    def own_tile(b):
        return w.at[b, z % 4, z // 4] if b == 5 else w.at[b, z % 4, z // 4, x]

    def own_class(b, part):
        return w.at[b, z % 4, part] if b == 5 else w.at[b, z % 4, part, x]

    def tiles(b, n):
        if n in (7, 8, 15):
            return vw.at[pl.ds(0, n), pl.ds(0, 16)]
        if n == 3:
            return w.at[b, 0, 0, pl.ds(0, 3)]
        if n == 12:
            return w.at[b, 0, pl.ds(0, 3)]
        return w.at[b, pl.ds(0, n // 16)]

    def along_x(i):
        return {"tm": z_hi * 8 + ((x + i) % 4) * 2 + core}

    def send_far(b):
        for i in FAR:
            push(own_tile(b), z_s.at[b], far_r.at[b], **along_z(i))

    def send_close():
        for i in CLOSE:
            push(own_tile(0), z_s.at[0], near_r.at[0], **along_z(i))

    def send_apart():
        for i in APART:
            push(own_tile(0), z_s.at[0], far_r.at[0], **along_z(i))

    def pass_on(offsets):
        for i in offsets:
            at = (z + Z - i) % Z
            ref = w.at[0, at % 4, at // 4, x]
            for k in (2, 1, 3):
                push(ref, x_s.at[0], x_r.at[0], **along_x(k))

    def all_over_x():
        arrived(tiles(0, 8), near_r.at[0])
        pass_on((0,) + CLOSE)
        arrived(tiles(0, 7), far_r.at[0])
        pass_on(APART)
        push(column(0, 0), sib_s.at[0], sib_r.at[0], tm=twin)

    def send_near(b):
        arrived(tiles(b, 12 if b == 5 else 3), far_r.at[b])
        for i, part in NEAR.items():
            push(own_class(b, part), z_s.at[6 if b == 5 else b], near_r.at[b], **along_z(i))

    def column(b, i):
        return w.at[b, :, :, (x + 4 - i) % 4]

    def send_x(b):
        arrived(tiles(b, 12), near_r.at[b])
        for i in (2, 1, 3):
            push(column(b, 0), x_s.at[b], x_r.at[b], **along_x(i))
        push(column(b, 0), sib_s.at[b], sib_r.at[b], tm=twin)

    def send_twin(b):
        arrived(tiles(b, 48), x_r.at[b])
        for i in (1, 3, 2):
            push(column(b, i), sib_s.at[b], sib_r.at[b], tm=twin)

    def first_x():
        ref = w.at[5, z % 4, z // 4, x]
        for i in (2, 1, 3):
            push(ref, x_s.at[5], x_r.at[5], **along_x(i))

    def far_5():
        arrived(tiles(5, 3), x_r.at[5])
        send_far(5)

    def twin_5():
        arrived(tiles(5, 48), near_r.at[5])
        push(w.at[5], sib_s.at[5], sib_r.at[5], tm=twin)

    def from_twin(b):
        arrived(w.at[b], sib_r.at[b])

    @on(0)
    def _():
        send_close()

    halo_copy.wait_recv()
    wbuf[320:328] = jnp.where(position[320:328] < length, halo[...], 0.0)
    log_mel(56, 8, (2, 3))
    row = lax.broadcasted_iota(jnp.int32, (256, MEL), 0)
    valid_mel = seg * 256 + (row % 64) * 4 + row // 64 < length // HOP
    log_energy = jnp.concatenate([lg[j] for j in range(STRIDE)], axis=0)
    kept = jnp.where(valid_mel, log_energy, 0.0)
    place = z_hi * 4 + mp
    ma[place] = jnp.concatenate(
        [
            jnp.sum(kept, axis=0, keepdims=True),
            jnp.sum(kept * kept, axis=0, keepdims=True),
            jnp.zeros((6, MEL), F32),
        ],
        axis=0,
    )

    for i in (4, 5, 6, 7, 3, 2, 1):
        away = (place + i) % 8
        push(ma.at[place], ma_s, ma_r, tm=(away // 4) * 8 + q, mp=away % 4)

    @on(0)
    def _():
        send_apart()
        send_far(1)
        send_far(2)

    @on(1)
    def _():
        first_x()
        send_far(3)
        send_far(4)

    own = pl.ds(pl.multiple_of(8 + mp * 64, 8), 64)
    for j in range(STRIDE):
        le[j, own, :] = log_energy[j * 64 : j * 64 + 64]

    ours = le.at[:, own, :]
    next_halo = le.at[:, pl.ds(256, 8), :], le.at[:, pl.ds(0, 8), :]

    @pl.when(mp == 3)
    def _():
        for i in range(4):
            remote(*next_halo, lh_s, lh_r, tm=tm_up, mp=(mp + i) % 4).start()

    for i in (2, 1, 3):
        push(ours, le_s, le_r, mp=(mp + i) % 4)
    arrived(ma.at[pl.ds(0, 7)], ma_r)
    total = ma[0]
    for i in range(1, 8):
        total = total + ma[i]
    mb[q] = total
    for i in range(1, 8):
        push(mb.at[q], mb_s, mb_r, tm=z_hi * 8 + (q + i) % 8)

    @on(0)
    def _():
        all_over_x()
        send_near(1)
        send_near(2)

    @on(1)
    def _():
        far_5()
        send_near(3)
        send_near(4)
        send_x(3)

    arrived(mb.at[pl.ds(0, 7)], mb_r)
    total = mb[0]
    for i in range(1, 8):
        total = total + mb[i]
    count = (length // HOP).astype(F32)
    mel_mean = total[0:1] / count
    mel_var = total[1:2] / count - mel_mean * mel_mean
    mel_scale = lax.rsqrt(mel_var + 1e-05)
    arrived(le.at[:, pl.ds(0, 192), :], le_r)
    arrived(le.at[:, pl.ds(0, 8), :], lh_r)
    time = tm * 256 - 8 + lax.broadcasted_iota(jnp.int32, (264, MEL), 0)
    for j in range(STRIDE):
        known = (time >= 0) & (time * 4 + j < length // HOP)
        nmf[j] = jnp.where(known, (le[j] - mel_mean) * mel_scale, 0.0)

    @on(0)
    def _():
        send_twin(0)

    @on(1)
    def _():
        send_near(5)
        send_x(4)
        from_twin(0)

    for s in range(Z):
        for i in range(4):
            at = (s % 2) * 8 + s // 2
            sf[56 * s + 14 * i : 56 * s + 14 * i + 14, :] = w[0, at % 4, at // 4, i].astype(
                F32
            )[0:14]
    stacked = jnp.concatenate(
        [nmf[j, 7:263] for j in range(1, STRIDE)] + [nmf[j, 8:264] for j in range(STRIDE)],
        axis=1,
    ).astype(BF16)
    feats[mp] = jnp.dot(
        stacked, sf[...].astype(BF16), preferred_element_type=F32
    ).astype(BF16)

    for half in range(2):
        rows = feats.at[mp, pl.ds(128 * half, 128)]
        for i in (2, 1, 3):
            push(rows, ag_s, ag_r.at[half], mp=(mp + i) % 4)

    @on(0)
    def _():
        send_x(1)
        from_twin(5)
        from_twin(3)
        send_x(2)

    @on(1)
    def _():
        twin_5()
        send_twin(3)
        send_twin(4)

    def layer_norm(b):
        rows = pl.ds(pl.multiple_of(b * 32, 32), 32)
        wide = jnp.concatenate([feats[g, rows, :] for g in range(4)], axis=1).astype(F32)
        centered = wide - jnp.mean(wide, axis=1, keepdims=True)
        spread = jnp.mean(centered * centered, axis=1, keepdims=True)
        normed[rows, :] = (centered * lax.rsqrt(spread + 1e-05)).astype(BF16)

    for half in range(2):
        arrived(feats.at[pl.ds(0, 3), pl.ds(0, 128)], ag_r.at[half])
        pl.loop(4 * half, 4 * half + 4, unroll=2)(layer_norm)

    @on(0)
    def _():
        from_twin(4)

    @pl.loop(0, Z)
    def _(s):
        value, gate = [], []
        at = (s % 2) * 8 + s // 2
        for i in range(4):
            top, middle, bottom = (
                w[b, at % 4, at // 4, i].astype(F32) for b in (3, 4, 5)
            )
            value += [top, middle[0:8]]
            gate += [middle[8:16], bottom]
        vw[s] = jnp.concatenate(value, axis=0).astype(BF16)
        gw[s] = jnp.concatenate(gate, axis=0).astype(BF16)

    value_sum = jnp.dot(
        normed[...], vw[...].reshape(1536, 384), preferred_element_type=F32
    )
    gate_sum = jnp.dot(
        normed[...], gw[...].reshape(1536, 384), preferred_element_type=F32
    )
    valid = (
        tm * 256 + lax.broadcasted_iota(jnp.int32, (256, 384), 0)
        < length // (STRIDE * HOP)
    )
    gated = jnp.where(valid, value_sum * jax.nn.sigmoid(gate_sum), 0.0)
    gp[16:272, :] = gated.astype(BF16)

    to_next = remote(
        gp.at[pl.ds(256, 16)], gp.at[pl.ds(0, 16)], gh_s.at[0], gh_r.at[0], tm=tm_up
    )
    to_prev = remote(
        gp.at[pl.ds(16, 16)], gp.at[pl.ds(272, 16)], gh_s.at[1], gh_r.at[1], tm=tm_down
    )
    to_next.start()
    to_prev.start()
    gf[16:272, :] = gp[16:272, :].astype(F32)
    loads[3].wait()

    def depthwise(block, column):
        rows = pl.multiple_of(block * 64, 64)
        lanes = pl.ds(pl.multiple_of(column * 128, 128), 128)
        window = gf[pl.ds(rows, 96), lanes]
        taps = dk[:, lanes]
        out = jnp.zeros((64, 128), F32)
        for p in range(8):
            part = jnp.zeros((72, 128), F32)
            for k in range(4):
                tap = 8 * k + p - 1
                if tap >= 0:
                    part = part + taps[tap : tap + 1] * window[8 * k : 8 * k + 72]
            if p:
                part = pltpu.roll(part, 72 - p, 0)
            out = out + part[:64]
        moved = out * scale[lanes].reshape(1, 128) + shift[lanes].reshape(1, 128)
        act[pl.ds(rows, 64), lanes] = (moved * jax.nn.sigmoid(moved)).astype(BF16)

    @pl.loop(0, 6)
    def _(b):
        depthwise(b // 3 + 1, b % 3)

    @on(0)
    def _():
        send_twin(1)
        send_twin(2)

    @on(1)
    def _():
        from_twin(1)
        from_twin(2)

    @pl.loop(0, Z)
    def _(s):
        rows = []
        at = (s % 2) * 8 + s // 2
        for i in range(4):
            rows += [
                w[1, at % 4, at // 4, i].astype(F32),
                w[2, at % 4, at // 4, i].astype(F32)[0:8],
            ]
        ow[s] = jnp.concatenate(rows, axis=0).astype(BF16)

    def partial(rows, g):
        block = ow[pl.ds(g * 4, 4)].reshape(384, 384)
        return lax.dot_general(
            rows, block, NT, preferred_element_type=F32
        ).astype(BF16)

    def scatter(i, start, rows):
        part = pl.ds(start, rows)
        remote(
            ps.at[i, part], rs.at[i, part], rs_s, rs_r, mp=(mp + i) % 4
        ).start()

    inner = act[64:192, :]
    for i in (2, 1, 3):
        ps[i, 64:192] = partial(inner, (mp + i) % 4)
        scatter(i, 64, 128)

    to_next.wait_recv()
    to_prev.wait_recv()
    gf[0:16, :] = jnp.where(tm == 0, 0.0, gp[0:16, :].astype(F32))
    gf[272:288, :] = jnp.where(tm == 15, 0.0, gp[272:288, :].astype(F32))

    @pl.loop(0, 6)
    def _(b):
        depthwise((b // 3) * 3, b % 3)

    outer = jnp.concatenate([act[0:64, :], act[192:256, :]], axis=0)
    for i in (2, 1, 3):
        part = partial(outer, (mp + i) % 4)
        ps[i, 0:64] = part[0:64]
        ps[i, 192:256] = part[64:128]
        scatter(i, 0, 64)
        scatter(i, 192, 64)
    summed = partial(act[...], mp).astype(F32)
    arrived(rs.at[pl.ds(1, 3)], rs_r)
    for i in range(1, 4):
        summed = summed + rs[i].astype(F32)
    out_ref[...] = jnp.where(valid, feats[mp].astype(F32) + summed, 0.0).astype(BF16)

    halo_copy.wait_send()
    swap.wait_send()
    left(ma.at[pl.ds(0, 7)], ma_s)
    left(mb.at[pl.ds(0, 7)], mb_s)
    left(le.at[:, pl.ds(0, 192), :], le_s)
    left(feats.at[pl.ds(0, 3)], ag_s)
    left(rs.at[pl.ds(1, 3)], rs_s)

    @pl.when(mp == 3)
    def _():
        left(le.at[:, pl.ds(0, 32), :], lh_s)

    to_next.wait_send()
    to_prev.wait_send()

    for c in range(2):
        @on(c)
        def _(c=c):
            for b in range(3 * c, 3 * c + 3):
                if b == 5:
                    left(tiles(b, 12), z_s.at[b])
                    left(tiles(b, 48), z_s.at[6])
                    left(tiles(b, 3), x_s.at[b])
                else:
                    left(tiles(b, 15), z_s.at[b])
                    left(tiles(b, 48), x_s.at[b])
                left(w.at[b], sib_s.at[b])


def shards(
    waveform, lengths, sub_weight, value_weight, gate_weight, out_weight,
    depth_kernel, norm_scale, norm_shift,
):
    vmem = pl.BlockSpec(memory_space=pltpu.VMEM)
    hbm = pl.BlockSpec(memory_space=pltpu.HBM)
    dma = pltpu.SemaphoreType.DMA
    encoded = pl.pallas_call(
        kernel,
        out_shape=pltpu.VMEM((256, 384), BF16),
        in_specs=[pl.BlockSpec(memory_space=pltpu.SMEM)] + [vmem] * 4 + [hbm] * 2 + [vmem] * 2 + [hbm] * 2,
        out_specs=vmem,
        scratch_shapes=[
            pltpu.VMEM((320, 128), F32),
            pltpu.VMEM((KERNEL, 384), F32),
            pltpu.VMEM((512, 512), F32),
            pltpu.VMEM((256, MEL), F32),
            pltpu.VMEM((328, 128), F32),
            pltpu.VMEM((8, 128), F32),
            pltpu.VMEM((4, 64, 128), F32),
            pltpu.VMEM((2, 32, 384), BF16),
            pltpu.VMEM((2, 32, 384), F32),
            pltpu.VMEM((32, 384), BF16),
            pltpu.VMEM((48, 384), F32),
            pltpu.VMEM((6, 4, 4, 4, 16, 384), BF16),
            pltpu.VMEM((896, 384), F32),
            pltpu.VMEM((Z, 96, 384), BF16),
            pltpu.VMEM((Z, 96, 384), BF16),
            pltpu.VMEM((Z, 96, 384), BF16),
            pltpu.VMEM((8, 8, 128), F32),
            pltpu.VMEM((8, 8, 128), F32),
            pltpu.VMEM((4, 264, 128), F32),
            pltpu.VMEM((4, 264, 128), F32),
            pltpu.VMEM((4, 256, 384), BF16),
            pltpu.VMEM((256, 1536), BF16),
            pltpu.VMEM((288, 384), BF16),
            pltpu.VMEM((288, 384), F32),
            pltpu.VMEM((256, 384), BF16),
            pltpu.VMEM((4, 256, 384), BF16),
            pltpu.VMEM((4, 256, 384), BF16),
            dma((4,)),
            dma, dma,
            dma, dma,
            dma, dma,
            dma, dma,
            dma, dma,
            dma, dma,
            dma, dma((2,)),
            dma((2,)), dma((2,)),
            dma, dma,
            dma((7,)), dma((6,)), dma((6,)),
            dma((6,)), dma((6,)),
            dma((6,)), dma((6,)),
        ],
        compiler_params=pltpu.CompilerParams(
            collective_id=0, has_side_effects=True, vmem_limit_bytes=60 * 1024 * 1024
        ),
    )(
        lengths,
        sub_weight,
        value_weight,
        gate_weight,
        out_weight.T,
        waveform.reshape(320, 128),
        depth_kernel,
        norm_scale,
        norm_shift,
        jnp.asarray(fourier_table()),
        jnp.asarray(mel_filters()),
    )
    return encoded[None]


def solution(mesh):
    placed = (
        P("dp", ("tm", "mp")),
        P("dp"),
        P(("dp", "tm"), "mp"),
        P(("dp", "tm"), "mp"),
        P(("dp", "tm"), "mp"),
        P("mp", ("dp", "tm")),
        P(None, "mp"),
        P("mp"),
        P("mp"),
    )
    return jax.shard_map(
        shards, mesh=mesh, in_specs=placed, out_specs=P("dp", "tm", "mp"), check_vma=False
    )
```
